256 devices in a mesh: term: 16 (over z, y_hi), sector: 16 (over x, y_lo, core).
Axes of the slice: x: 4, y: 4 (y_hi: 2, y_lo: 2; y = y_hi * 2 + y_lo), z: 8, core: 2. Of those that a mesh axis runs over, the one named last changes fastest.
Arguments:
- psi: bfloat16 [64, 128, 128], P('sector', 'term'), may hold values from -75 to 75
- diag_energy: float32 [64, 128, 128], P('sector', 'term'), may hold values from -4 to 6
- block_shape: int32 [64, 2], P('sector'), may hold values from 32 to 128
- env_left: bfloat16 [16, 16, 32, 128, 128], P('term', 'sector'), may hold values from -0.5 to 0.5
- env_right: bfloat16 [16, 16, 32, 128, 128], P('term', 'sector'), may hold values from -0.5 to 0.5
- pair_src: int32 [16, 16, 384], P('term', 'sector'), may hold values from 0 to 63
- pair_dst: int32 [16, 16, 384], P('term', 'sector'), may hold values from 0 to 3
- pair_left: int32 [16, 16, 384], P('term', 'sector'), may hold values from 0 to 31
- pair_right: int32 [16, 16, 384], P('term', 'sector'), may hold values from 0 to 31
- pair_count: int32 [16, 16], P('term', 'sector'), may hold values from 48 to 384, as said below
Outputs:
- sigma_one: float32 [64, 128, 128], P('sector', 'term')
- sigma_two: float32 [64, 128, 128], P('sector', 'term')
The draws below stay inside these ranges and needn't reach their ends.
Inputs may be any that keep to these rules, and one draw needn't show every extreme that they name: The live slots of the device at term index t and sector index s are slots 0 to pair_count[t, s] - 1; some device has all 384 slots live. A slot of sector index s adds to the global block s * 4 + pair_dst.
All inputs are finite; a program needn't handle non-finite values.
Results may differ from the reference program's by a relative error of at most 0.006.
Values may be sent and summed in bfloat16 or wider, within the bound.
A program may use at most 64 MiB of HBM per device.

```python
import math
import jax
import jax.numpy as jnp
from jax import lax

TILE = 128
BLK_DEV = 4
PAIRS = 384
ENV = 32
NBLK = 64
N_TERM = 16
N_SECTOR = 16


def draw_psi(key, part):
    key = jax.random.fold_in(key, 7)
    key_base, key_rows, key_cols = jax.random.split(key, 3)
    shape = (NBLK, TILE, TILE)
    base_noise = jnp.clip(jax.random.normal(key_base, shape, jnp.float32), -3.6, 3.6) + 0.4
    block_ids = jnp.arange(NBLK, dtype=jnp.float32)
    block_ramp = 0.6 * jnp.power(3.0, block_ids / max(NBLK - 1, 1))
    row_ids = jnp.arange(TILE, dtype=jnp.float32)
    row_ramp = jnp.power(3.0, 0.5 * row_ids / max(TILE - 1, 1))
    row_scale = jnp.exp(jax.random.uniform(key_rows, (NBLK, TILE, 1), jnp.float32, 0.0, math.log(10.0))) / math.sqrt(10.0)
    col_scale = jnp.exp(jax.random.uniform(key_cols, (NBLK, 1, TILE), jnp.float32, 0.0, math.log(10.0))) / math.sqrt(10.0)
    values = base_noise * block_ramp[:, None, None] * row_ramp[None, :, None] * row_scale * col_scale / 1.7
    return values.astype(jnp.bfloat16)


def draw_diag_energy(key, part):
    key = jax.random.fold_in(key, 9)
    key_level, key_noise = jax.random.split(key)
    shape = (NBLK, TILE, TILE)
    levels = jax.random.uniform(key_level, (NBLK, 1, 1), jnp.float32, -1.0, 2.0)
    noise_part = 0.5 * jnp.clip(jax.random.normal(key_noise, shape, jnp.float32), -4.0, 4.0)
    return (levels + noise_part).astype(jnp.float32)


def environment_tiles(key):
    shape = (N_TERM, N_SECTOR, ENV, TILE, TILE)
    spread = (BLK_DEV / (PAIRS * N_TERM)) ** 0.25 / math.sqrt(TILE)
    common = 4.0 / (TILE * math.sqrt(PAIRS * N_TERM / BLK_DEV))
    values = jnp.clip(jax.random.normal(key, shape, jnp.float32), -5.0, 5.0) * spread + common
    return values.astype(jnp.bfloat16)


def draw_env_left(key, part):
    key = jax.random.fold_in(key, 11)
    return environment_tiles(key)


def draw_env_right(key, part):
    key = jax.random.fold_in(key, 13)
    return environment_tiles(key)


def draw_pair_count(key, part):
    key = jax.random.fold_in(key, 5)
    key_load, key_full = jax.random.split(key)
    members = N_TERM * N_SECTOR
    ramp_draw = jax.random.randint(key_load, (members,), 0, 64)
    low_count = PAIRS // 8
    loads = low_count + (PAIRS - low_count) * ramp_draw * ramp_draw // 3969
    chosen = jax.random.randint(key_full, (), 0, members)
    flat_counts = jnp.where(jnp.arange(members, dtype=jnp.int32) == chosen, PAIRS, loads)
    return flat_counts.reshape(N_TERM, N_SECTOR).astype(jnp.int32)


def place_ends(result, stream_key, low, top_value):
    longest = result.shape.index(max(result.shape))
    spots = []
    for shift in (0, 1):
        where = [jax.random.randint(jax.random.fold_in(stream_key, axis), (), 0, length) for axis, length in enumerate(result.shape)]
        where[longest] = (where[longest] + shift) % result.shape[longest]
        spots.append(tuple(where))
    return result.at[spots[0]].set(low).at[spots[1]].set(top_value)


def setup_inputs(seed: int = 0) -> dict:
    seeds = jax.random.split(jax.random.key(seed), 11)
    return {
        "psi": draw_psi(jax.random.fold_in(seeds[10], 71), 0),
        "diag_energy": draw_diag_energy(jax.random.fold_in(seeds[10], 71), 0),
        "block_shape": place_ends(jax.random.randint(seeds[2], (NBLK, 2), TILE // 4, TILE + 1), jax.random.fold_in(seeds[2], 1), TILE // 4, TILE).astype(jnp.int32),
        "env_left": draw_env_left(jax.random.fold_in(seeds[10], 71), 0),
        "env_right": draw_env_right(jax.random.fold_in(seeds[10], 71), 0),
        "pair_src": place_ends(jax.random.randint(seeds[5], (N_TERM, N_SECTOR, PAIRS), 0, NBLK), jax.random.fold_in(seeds[5], 1), 0, NBLK - 1).astype(jnp.int32),
        "pair_dst": place_ends(jax.random.randint(seeds[6], (N_TERM, N_SECTOR, PAIRS), 0, BLK_DEV), jax.random.fold_in(seeds[6], 1), 0, BLK_DEV - 1).astype(jnp.int32),
        "pair_left": place_ends(jax.random.randint(seeds[7], (N_TERM, N_SECTOR, PAIRS), 0, ENV), jax.random.fold_in(seeds[7], 1), 0, ENV - 1).astype(jnp.int32),
        "pair_right": place_ends(jax.random.randint(seeds[8], (N_TERM, N_SECTOR, PAIRS), 0, ENV), jax.random.fold_in(seeds[8], 1), 0, ENV - 1).astype(jnp.int32),
        "pair_count": draw_pair_count(jax.random.fold_in(seeds[10], 71), 0),
    }


def valid_region(block_shape):
    row_ids = jnp.arange(TILE, dtype=jnp.int32)
    return (row_ids[None, :, None] < block_shape[:, 0, None, None]) & (row_ids[None, None, :] < block_shape[:, 1, None, None])

def apply_terms(vector, env_left, env_right, pair_src, pair_dst, pair_left, pair_right, pair_count):
    members = N_TERM * N_SECTOR
    lefts = env_left.reshape(members, ENV, TILE, TILE)
    rights = env_right.reshape(members, ENV, TILE, TILE)
    sources = pair_src.reshape(members, PAIRS)
    targets = pair_dst.reshape(members, PAIRS)
    left_sel = pair_left.reshape(members, PAIRS)
    right_sel = pair_right.reshape(members, PAIRS)
    counts = pair_count.reshape(members)

    def one_member(inputs):
        left_tiles, right_tiles, source_ids, target_ids, left_ids, right_ids, live_count = inputs
        moved = vector[source_ids].astype(jnp.float32)
        left_ops = left_tiles[left_ids].astype(jnp.float32)
        right_ops = right_tiles[right_ids].astype(jnp.float32)
        left_half = jnp.einsum('pxk,pky->pxy', left_ops, moved).astype(jnp.bfloat16)
        left_half = lax.optimization_barrier(left_half).astype(jnp.float32)
        product = jnp.einsum('pxk,pky->pxy', left_half, right_ops)
        live_slots = (jnp.arange(PAIRS, dtype=jnp.int32) < live_count).astype(jnp.float32)
        onehot = (target_ids[:, None] == jnp.arange(BLK_DEV, dtype=jnp.int32)[None, :]).astype(jnp.float32)
        onehot = onehot * live_slots[:, None]
        return jnp.einsum('pb,pxy->bxy', onehot, product)
    partials = lax.map(one_member, (lefts, rights, sources, targets, left_sel, right_sel, counts))
    return partials.reshape(N_TERM, N_SECTOR * BLK_DEV, TILE, TILE).sum(axis=0)

def reference(psi, diag_energy, block_shape, env_left, env_right, pair_src, pair_dst, pair_left, pair_right, pair_count):
    inside = valid_region(block_shape)
    start = jnp.where(inside, psi, jnp.zeros_like(psi))
    start_f = start.astype(jnp.float32)
    coupled = apply_terms(start, env_left, env_right, pair_src, pair_dst, pair_left, pair_right, pair_count)
    sigma_one = jnp.where(inside, diag_energy * start_f + coupled, jnp.float32(0.0))
    rayleigh = jnp.sum(start_f * sigma_one) / jnp.sum(start_f * start_f)
    residual = sigma_one - rayleigh * start_f
    second = (residual * lax.rsqrt(jnp.mean(residual * residual) + 1e-06)).astype(jnp.bfloat16)
    coupled_two = apply_terms(second, env_left, env_right, pair_src, pair_dst, pair_left, pair_right, pair_count)
    sigma_two = jnp.where(inside, diag_energy * second.astype(jnp.float32) + coupled_two, jnp.float32(0.0))
    return (sigma_one, sigma_two)
```

```python
import functools

import jax
import jax.numpy as jnp
from jax import lax
from jax.experimental import pallas as pl
from jax.experimental.pallas import tpu as pltpu
from jax.sharding import PartitionSpec as P

F32 = jnp.float32
BF16 = jnp.bfloat16
I32 = jnp.int32
MESH = pl.DeviceIdType.MESH

TILE = 128
PAIRS = 384
ENV = 32
BLK = 4
ROWS = 8
NX, NY, NZ, NCORE = 4, 4, 8, 2
N_TERM, N_SECTOR = 16, 16
NBLK = N_SECTOR * BLK
GROUPS = ENV * BLK
UNROLL = 32
N_SEND = 160
NT = (((1,), (1,)), ((), ()))


def dot(a, b):
    return jnp.dot(a, b, preferred_element_type=F32)


def as_bf16(flags):
    return flags.astype(F32).astype(BF16)


def schedule(source, target, left, right, count, steps_ref, last_ref):
    slot = lax.broadcasted_iota(I32, (1, PAIRS), 1)
    live = slot < count
    key = jnp.where(live, left * BLK + target, GROUPS)
    member = lax.broadcasted_iota(I32, (GROUPS, PAIRS), 0) == key
    member_f = member.astype(F32)
    member_b = member_f.astype(BF16)
    earlier = as_bf16(
        lax.broadcasted_iota(I32, (PAIRS, PAIRS), 0) < lax.broadcasted_iota(I32, (PAIRS, PAIRS), 1)
    )
    rank = jnp.sum(member_f * dot(member_b, earlier), axis=0, keepdims=True)
    row_g = lax.broadcasted_iota(I32, (GROUPS, GROUPS), 0)
    col_g = lax.broadcasted_iota(I32, (GROUPS, GROUPS), 1)
    size = jnp.broadcast_to(jnp.sum(member_f, axis=1, keepdims=True), (GROUPS, GROUPS))
    high = jnp.floor(size * (1.0 / 16.0))
    low = size - 16.0 * high
    below = as_bf16(col_g < row_g)
    begin = 16.0 * dot(below, high.astype(BF16)) + dot(below, low.astype(BF16))
    begin_of = jnp.sum(member_f * begin[:, :1], axis=0, keepdims=True)
    place = jnp.where(live, (rank + begin_of).astype(I32), -1)
    sent = as_bf16(lax.broadcasted_iota(I32, (PAIRS, PAIRS), 0) == place)
    line = lax.broadcasted_iota(I32, (8, PAIRS), 0)
    table = jnp.where(line == 0, source, jnp.where(line == 1, right, jnp.where(line == 2, key, 0)))
    moved = lax.dot_general(table.astype(F32).astype(BF16), sent, NT, preferred_element_type=F32)
    again = (moved == pltpu.roll(moved, 1, 1)) & (lax.broadcasted_iota(I32, (8, PAIRS), 1) > 0)
    top = jnp.where(line == 0, NBLK - 1, jnp.where(line == 1, ENV - 1, 1))
    steps_ref[...] = jnp.clip(jnp.where(line == 2, again.astype(I32), moved.astype(I32)), 0, top)
    size = lax.dot_general(jnp.ones((8, PAIRS), BF16), member_b, NT, preferred_element_type=F32)
    high = jnp.floor(size * (1.0 / 16.0))
    low = size - 16.0 * high
    above = as_bf16(row_g < col_g)
    begin = 16.0 * dot(high.astype(BF16), above) + dot(low.astype(BF16), above)
    ends = (begin + size).astype(I32) - 1
    last_ref[...] = jnp.where(size > 0.5, jnp.clip(ends, 0, PAIRS - 1), PAIRS)


def contract(steps, last, vector, lefts, rights, prefix, total):
    def step_body(turn, running):
        for u in range(UNROLL):
            k = turn * UNROLL + u
            keep = steps[2, k].astype(F32)
            running = running * keep + dot(vector[steps[0, k]], rights[steps[1, k]])
            prefix[k] = running.astype(BF16)
        return running

    lax.fori_loop(0, PAIRS // UNROLL, step_body, jnp.zeros((TILE, TILE), F32))
    for half in range(2):

        def left_body(turn, running):
            for u in range(4):
                l = (turn * 4 + u) * 2
                tiles = jnp.concatenate([lefts[l], lefts[l + 1]], axis=1)
                sums = [
                    jnp.concatenate(
                        [prefix[last[0, (l + dl) * BLK + half * 2 + db]] for db in range(2)], axis=1
                    )
                    for dl in range(2)
                ]
                running = running + dot(tiles, jnp.concatenate(sums, axis=0))
            return running

        both = lax.fori_loop(0, ENV // 8, left_body, jnp.zeros((TILE, 2 * TILE), F32))
        total[half * 2] = both[:, :TILE]
        total[half * 2 + 1] = both[:, TILE:]


def device_of(x, y, z, core):
    return (z * 2 + lax.div(y, 2), x * 4 + lax.rem(y, 2) * 2 + core)


class Links:
    def __init__(self, send_sem, recv_sem):
        self.send_sem, self.recv_sem = send_sem, recv_sem
        self.used = 0
        self.started = []

    def slot(self):
        self.used += 1
        return self.used - 1

    def copy(self, ref, slot, device, dst=None):
        return pltpu.make_async_remote_copy(
            src_ref=ref,
            dst_ref=ref if dst is None else dst,
            send_sem=self.send_sem.at[slot],
            recv_sem=self.recv_sem.at[slot],
            device_id=device,
            device_id_type=MESH,
        )

    def send(self, ref, slot, device, dst=None):
        copy = self.copy(ref, slot, device, dst)
        copy.start()
        self.started.append(copy)

    def arrived(self, ref, slot, device):
        self.copy(ref, slot, device).wait_recv()

    def drain(self):
        for copy in self.started:
            copy.wait_send()
        self.started = []


def gather(links, raw, at, meanwhile):
    x, y, z, core = at
    mate = device_of(x, y, z, 1 - core)

    def along(axis, step):
        if axis == "x":
            return device_of(lax.rem(x + step + NX, NX), y, z, core)
        return device_of(x, lax.rem(y + step + NY, NY), z, core)

    slots = [links.slot() for _ in range(1, NZ)]
    for d in (4, 3, 5, 2, 6, 1, 7):
        to = device_of(x, y, lax.rem(z + d, NZ), core)
        links.send(raw.at[:, core, x, y, z], slots[d - 1], to)
    meanwhile()
    for d in range(1, NZ):
        begin = lax.rem(z - d + NZ, NZ)
        links.arrived(raw.at[:, core, x, y, begin], slots[d - 1], device_of(x, y, begin, core))

    handed = []

    def hand(pick):
        slot = links.slot()
        links.send(pick(core), slot, mate)
        handed.append((pick, slot))

    class Ring:
        def __init__(self, axis, pick, parts):
            self.axis, self.pick, self.parts = axis, pick, parts
            self.here = x if axis == "x" else y
            self.slots = [links.slot() for _ in range(4)]

        def index(self, step):
            return lax.rem(self.here + step + 4, 4)

        def start(self):
            links.send(self.pick(core, self.here), self.slots[0], along(self.axis, 1))
            links.send(self.pick(core, self.here), self.slots[1], along(self.axis, -1))

        def relay(self, side):
            piece = self.index(side)
            back = 0 if side == -1 else 1
            links.arrived(self.pick(core, piece), self.slots[back], along(self.axis, side))
            half = self.parts(self.pick(core, piece), back)
            links.send(half, self.slots[2 + back], along(self.axis, -side))
            hand(lambda c: self.pick(c, piece))

        def finish(self):
            piece = self.index(2)
            for back, side in ((0, -1), (1, 1)):
                half = self.parts(self.pick(core, piece), back)
                links.arrived(half, self.slots[2 + back], along(self.axis, side))
            hand(lambda c: self.pick(c, piece))

    near = pl.ds(0, 4), pl.ds(4, 4)
    pair = pl.ds(0, 2), pl.ds(2, 2)
    hand(lambda c: raw.at[:, c, x, y])
    first = Ring("y", lambda c, i: raw.at[0, c, x, i], lambda ref, k: ref.at[near[k]])
    second = Ring("x", lambda c, i: raw.at[1, c, i, y], lambda ref, k: ref.at[near[k]])
    wide_first = Ring("x", lambda c, i: raw.at[0, c, i], lambda ref, k: ref.at[pair[k]])
    wide_second = Ring("y", lambda c, i: raw.at[1, c, :, i], lambda ref, k: ref.at[pair[k]])
    first.start()
    second.start()
    for side in (-1, 1):
        first.relay(side)
        second.relay(side)
    first.finish()
    wide_first.start()
    second.finish()
    wide_second.start()
    for side in (-1, 1):
        wide_first.relay(side)
        wide_second.relay(side)
    wide_first.finish()
    wide_second.finish()
    for pick, slot in handed:
        links.arrived(pick(1 - core), slot, mate)
    links.drain()


def settle(raw, vector):
    def body(turn, squares):
        h = lax.div(turn, 8)
        core = lax.rem(lax.div(turn, 4), 2)
        x = lax.rem(turn, 4)
        for y_lo in range(2):
            halves = [
                raw[h, core, x, y_hi * 2 + y_lo].astype(F32).reshape(NZ, 2, ROWS, TILE) for y_hi in range(2)
            ]
            for k in range(2):
                tile = jnp.stack([halves[0][:, k], halves[1][:, k]], axis=1)
                squares = squares + jnp.sum((tile * tile).reshape(2 * NZ, ROWS, TILE), axis=0)
                block = (x * 4 + y_lo * 2 + core) * BLK + h * 2 + k
                vector[block] = tile.reshape(TILE, TILE).astype(BF16)
        return squares

    return lax.fori_loop(0, 2 * NCORE * NX, body, jnp.zeros((ROWS, TILE), F32))


def spread(links, total, out, back, me, at_term):
    for h in range(2):
        rows = [total[h * 2 + k].reshape(N_TERM, ROWS, TILE) for k in range(2)]
        both = jnp.stack(rows, axis=1).reshape(N_TERM, 2 * ROWS, TILE).astype(BF16)
        out[:, h] = both
    slots = [links.slot() for _ in range(1, N_TERM)]
    for d in range(1, N_TERM):
        peer = lax.rem(me + d, N_TERM)
        links.send(out.at[peer], slots[d - 1], at_term(peer), back.at[d])
    return slots


def merge(links, slots, out, back, me, at_term):
    acc = out[me].astype(F32)
    for d in range(1, N_TERM):
        peer = lax.rem(me - d + N_TERM, N_TERM)
        links.arrived(back.at[d], slots[d - 1], at_term(peer))
        acc = acc + back[d].astype(F32)
    return acc.reshape(BLK, ROWS, TILE)


def everyone(links, mine, back, here, n, at):
    slots = [links.slot() for _ in range(1, n)]
    for d in range(1, n):
        links.send(mine, slots[d - 1], at(lax.rem(here + d, n)), back.at[d])

    def wait():
        acc = mine[...]
        for d in range(1, n):
            links.arrived(back.at[d], slots[d - 1], at(lax.rem(here - d + n, n)))
            acc = acc + back[d]
        return acc

    return wait


def kernel(
    psi,
    diag,
    shape,
    env_left,
    env_right,
    source,
    target,
    left,
    right,
    count,
    sigma_one,
    sigma_two,
    raw_one,
    raw_two,
    vector,
    lefts,
    rights,
    prefix,
    total,
    out_one,
    out_two,
    back_one,
    back_two,
    part,
    part_sector,
    part_term,
    steps_v,
    last_v,
    steps_s,
    last_s,
    local_sem,
    send_sem,
    recv_sem,
):
    term, sector = lax.axis_index("term"), lax.axis_index("sector")
    z, y_hi = lax.div(term, 2), lax.rem(term, 2)
    x, y_lo, core = lax.div(sector, 4), lax.rem(lax.div(sector, 2), 2), lax.rem(sector, 2)
    y = y_hi * 2 + y_lo
    at = (x, y, z, core)

    def at_term(t):
        return (t, sector)

    def at_sector(s):
        return (term, s)

    barrier = pltpu.get_barrier_semaphore()
    greeted = [at_term(lax.rem(term + d, N_TERM)) for d in range(1, N_TERM)]
    greeted += [at_sector(lax.rem(sector + d, N_SECTOR)) for d in range(1, N_SECTOR)]
    greeted += [(z * 2 + 1 - y_hi, x * 4 + (1 - y_lo) * 2 + core)]
    for device in greeted:
        pl.semaphore_signal(barrier, inc=1, device_id=device, device_id_type=MESH)

    fetch_left = pltpu.make_async_copy(env_left.at[0, 0], lefts, local_sem.at[0])
    fetch_right = pltpu.make_async_copy(env_right.at[0, 0], rights, local_sem.at[1])
    fetch_left.start()
    fetch_right.start()

    row = lax.broadcasted_iota(I32, (ROWS, TILE), 0) + term * ROWS
    col = lax.broadcasted_iota(I32, (ROWS, TILE), 1)
    inside = [(row < shape[b, 0]) & (col < shape[b, 1]) for b in range(BLK)]
    start = [jnp.where(inside[b], psi[b].astype(F32), 0.0) for b in range(BLK)]
    for h in range(2):
        raw_one[h, core, x, y, z] = jnp.concatenate(start[h * 2 : h * 2 + 2], axis=0).astype(BF16)
    prefix[PAIRS] = jnp.zeros((TILE, TILE), BF16)

    links = Links(send_sem, recv_sem)
    pl.semaphore_wait(barrier, len(greeted))

    def plan():
        schedule(source[0], target[0], left[0], right[0], count[0, 0], steps_v, last_v)
        copies = [
            pltpu.make_async_copy(steps_v, steps_s, local_sem.at[2]),
            pltpu.make_async_copy(last_v, last_s, local_sem.at[3]),
        ]
        for copy in copies:
            copy.start()
        for copy in copies:
            copy.wait()

    gather(links, raw_one, at, plan)
    start_squares = jnp.sum(settle(raw_one, vector), keepdims=True)
    fetch_left.wait()
    fetch_right.wait()
    contract(steps_s, last_s, vector, lefts, rights, prefix, total)

    overlap = jnp.zeros((ROWS, TILE), F32)
    for b in range(BLK):
        overlap = overlap + start[b] * start[b] * diag[b]
        both = vector[sector * BLK + b].astype(F32) * total[b]
        overlap = overlap + jnp.sum(both.reshape(TILE // ROWS, ROWS, TILE), axis=0)
    part[0] = overlap
    sector_sum = everyone(links, part.at[0], part_sector, sector, N_SECTOR, at_sector)
    slots = spread(links, total, out_one, back_one, term, at_term)
    part[1] = sector_sum()
    term_sum = everyone(links, part.at[1], part_term, term, N_TERM, at_term)
    coupled = merge(links, slots, out_one, back_one, term, at_term)
    sigma = [jnp.where(inside[b], diag[b] * start[b] + coupled[b], 0.0) for b in range(BLK)]
    for b in range(BLK):
        sigma_one[b] = sigma[b]
    rayleigh = jnp.sum(term_sum(), keepdims=True) / start_squares
    residual = [sigma[b] - rayleigh * start[b] for b in range(BLK)]
    for h in range(2):
        raw_two[h, core, x, y, z] = jnp.concatenate(residual[h * 2 : h * 2 + 2], axis=0).astype(BF16)
    links.drain()

    gather(links, raw_two, at, lambda: None)
    squares = jnp.sum(settle(raw_two, vector), keepdims=True)
    scale = lax.rsqrt(squares / float(NBLK * TILE * TILE) + 1e-06)
    contract(steps_s, last_s, vector, lefts, rights, prefix, total)
    slots = spread(links, total, out_two, back_two, term, at_term)
    coupled = merge(links, slots, out_two, back_two, term, at_term)
    for b in range(BLK):
        second = residual[b].astype(BF16).astype(F32)
        sigma_two[b] = jnp.where(inside[b], (diag[b] * second + coupled[b]) * scale, 0.0)
    links.drain()


def body(*args):
    vmem = pl.BlockSpec(memory_space=pltpu.VMEM)
    smem = pl.BlockSpec(memory_space=pltpu.SMEM)
    hbm = pl.BlockSpec(memory_space=pl.ANY)
    out = jax.ShapeDtypeStruct((BLK, ROWS, TILE), F32)
    raw = pltpu.VMEM((2, NCORE, NX, NY, NZ, 2 * ROWS, TILE), BF16)
    rows = pltpu.VMEM((N_TERM, 2, 2 * ROWS, TILE), BF16)
    return pl.pallas_call(
        kernel,
        out_shape=(out, out),
        in_specs=[vmem, vmem, smem, hbm, hbm, vmem, vmem, vmem, vmem, smem],
        out_specs=(vmem, vmem),
        scratch_shapes=[
            raw,
            raw,
            pltpu.VMEM((NBLK, TILE, TILE), BF16),
            pltpu.VMEM((ENV, TILE, TILE), BF16),
            pltpu.VMEM((ENV, TILE, TILE), BF16),
            pltpu.VMEM((PAIRS + 1, TILE, TILE), BF16),
            pltpu.VMEM((BLK, TILE, TILE), F32),
            rows,
            rows,
            rows,
            rows,
            pltpu.VMEM((2, ROWS, TILE), F32),
            pltpu.VMEM((N_SECTOR, ROWS, TILE), F32),
            pltpu.VMEM((N_TERM, ROWS, TILE), F32),
            pltpu.VMEM((8, PAIRS), I32),
            pltpu.VMEM((8, TILE), I32),
            pltpu.SMEM((8, PAIRS), I32),
            pltpu.SMEM((8, TILE), I32),
            pltpu.SemaphoreType.DMA((4,)),
            pltpu.SemaphoreType.DMA((N_SEND,)),
            pltpu.SemaphoreType.DMA((N_SEND,)),
        ],
        compiler_params=pltpu.CompilerParams(
            collective_id=0, has_side_effects=True, vmem_limit_bytes=48 * 2**20
        ),
        name="two_products",
    )(*args)


def solution(mesh):
    placed = (
        P("sector", "term", None),
        P("sector", "term", None),
        P("sector", None),
        P("term", "sector", None, None, None),
        P("term", "sector", None, None, None),
        P("term", "sector", None),
        P("term", "sector", None),
        P("term", "sector", None),
        P("term", "sector", None),
        P("term", "sector"),
    )
    return jax.shard_map(
        body,
        mesh=mesh,
        in_specs=placed,
        out_specs=(P("sector", "term", None), P("sector", "term", None)),
        check_vma=False,
    )
```

```python
import functools

import jax
import jax.numpy as jnp
from jax import lax
from jax.experimental import pallas as pl
from jax.experimental.pallas import tpu as pltpu
from jax.sharding import PartitionSpec as P

F32 = jnp.float32
BF16 = jnp.bfloat16
I32 = jnp.int32
MESH = pl.DeviceIdType.MESH

TILE = 128
PAIRS = 384
ENV = 32
BLK = 4
ROWS = 8
NX, NY, NZ, NCORE = 4, 4, 8, 2
N_TERM, N_SECTOR = 16, 16
NBLK = N_SECTOR * BLK
GROUPS = ENV * BLK
UNROLL = 32
N_SEND = 192
OFFSETS = (0, 1, -1, 2, -2, 3, -3, 4)
ZGROUPS = ((0, 3), (3, 7), (7, 8))
NT = (((1,), (1,)), ((), ()))


def dot(a, b):
    return jnp.dot(a, b, preferred_element_type=F32)


def as_bf16(flags):
    return flags.astype(F32).astype(BF16)


def schedule(source, target, left, right, count, steps_ref, last_ref):
    slot = lax.broadcasted_iota(I32, (1, PAIRS), 1)
    live = slot < count
    key = jnp.where(live, left * BLK + target, GROUPS)
    member = lax.broadcasted_iota(I32, (GROUPS, PAIRS), 0) == key
    member_f = member.astype(F32)
    member_b = member_f.astype(BF16)
    earlier = as_bf16(
        lax.broadcasted_iota(I32, (PAIRS, PAIRS), 0) < lax.broadcasted_iota(I32, (PAIRS, PAIRS), 1)
    )
    rank = jnp.sum(member_f * dot(member_b, earlier), axis=0, keepdims=True)
    row_g = lax.broadcasted_iota(I32, (GROUPS, GROUPS), 0)
    col_g = lax.broadcasted_iota(I32, (GROUPS, GROUPS), 1)
    size = jnp.broadcast_to(jnp.sum(member_f, axis=1, keepdims=True), (GROUPS, GROUPS))
    high = jnp.floor(size * (1.0 / 16.0))
    low = size - 16.0 * high
    below = as_bf16(col_g < row_g)
    begin = 16.0 * dot(below, high.astype(BF16)) + dot(below, low.astype(BF16))
    begin_of = jnp.sum(member_f * begin[:, :1], axis=0, keepdims=True)
    place = jnp.where(live, (rank + begin_of).astype(I32), -1)
    sent = as_bf16(lax.broadcasted_iota(I32, (PAIRS, PAIRS), 0) == place)
    line = lax.broadcasted_iota(I32, (8, PAIRS), 0)
    table = jnp.where(line == 0, source, jnp.where(line == 1, right, jnp.where(line == 2, key, 0)))
    moved = lax.dot_general(table.astype(F32).astype(BF16), sent, NT, preferred_element_type=F32)
    again = (moved == pltpu.roll(moved, 1, 1)) & (lax.broadcasted_iota(I32, (8, PAIRS), 1) > 0)
    top = jnp.where(line == 0, NBLK - 1, jnp.where(line == 1, ENV - 1, 1))
    steps_ref[...] = jnp.clip(jnp.where(line == 2, again.astype(I32), moved.astype(I32)), 0, top)
    size = lax.dot_general(jnp.ones((8, PAIRS), BF16), member_b, NT, preferred_element_type=F32)
    high = jnp.floor(size * (1.0 / 16.0))
    low = size - 16.0 * high
    above = as_bf16(row_g < col_g)
    begin = 16.0 * dot(high.astype(BF16), above) + dot(low.astype(BF16), above)
    ends = (begin + size).astype(I32) - 1
    last_ref[...] = jnp.where(size > 0.5, jnp.clip(ends, 0, PAIRS - 1), PAIRS)


def contract(steps, last, vector, lefts, rights, prefix, total):
    def step_body(turn, running):
        for u in range(UNROLL):
            k = turn * UNROLL + u
            keep = steps[2, k].astype(F32)
            tile = vector[steps[0, k]].reshape(TILE, TILE)
            running = running * keep + dot(tile, rights[steps[1, k]])
            prefix[k] = running.astype(BF16)
        return running

    lax.fori_loop(0, PAIRS // UNROLL, step_body, jnp.zeros((TILE, TILE), F32))
    for half in range(2):

        def left_body(turn, running):
            for u in range(4):
                l = (turn * 4 + u) * 2
                tiles = jnp.concatenate([lefts[l], lefts[l + 1]], axis=1)
                sums = [
                    jnp.concatenate(
                        [prefix[last[0, (l + dl) * BLK + half * 2 + db]] for db in range(2)], axis=1
                    )
                    for dl in range(2)
                ]
                running = running + dot(tiles, jnp.concatenate(sums, axis=0))
            return running

        both = lax.fori_loop(0, ENV // 8, left_body, jnp.zeros((TILE, 2 * TILE), F32))
        total[half * 2] = both[:, :TILE]
        total[half * 2 + 1] = both[:, TILE:]


def device_of(x, y, z, core):
    return (z * 2 + lax.div(y, 2), x * 4 + lax.rem(y, 2) * 2 + core)


class Links:
    def __init__(self, send_sem, recv_sem):
        self.send_sem, self.recv_sem = send_sem, recv_sem
        self.used = 0
        self.started = []

    def slot(self):
        self.used += 1
        return self.used - 1

    def copy(self, ref, slot, device, dst=None):
        return pltpu.make_async_remote_copy(
            src_ref=ref,
            dst_ref=ref if dst is None else dst,
            send_sem=self.send_sem.at[slot],
            recv_sem=self.recv_sem.at[slot],
            device_id=device,
            device_id_type=MESH,
        )

    def send(self, ref, slot, device, dst=None):
        copy = self.copy(ref, slot, device, dst)
        copy.start()
        self.started.append(copy)

    def arrived(self, ref, slot, device):
        self.copy(ref, slot, device).wait_recv()

    def drain(self):
        for copy in self.started:
            copy.wait_send()
        self.started = []


def gather(links, raw, vector, at, ready):
    x, y, z, core = at
    mate = device_of(x, y, z, 1 - core)
    squares = jnp.zeros((ROWS, TILE), F32)

    def wrap(i):
        return lax.rem(i, 4)

    def along_x(step):
        return device_of(wrap(x + step), y, z, core)

    def along_y(step):
        return device_of(x, wrap(y + step), z, core)

    def exchange(along, mine, theirs):
        slots = [links.slot() for _ in range(1, 4)]
        for d in (2, 1, 3):
            links.send(mine, slots[d - 1], along(d))

        def wait():
            for d in (1, 3, 2):
                links.arrived(theirs(4 - d), slots[d - 1], along(4 - d))

        return wait

    near, far, handed = [], [], []
    for begin, end in ZGROUPS:
        for k in range(begin, end):
            ready(k)
        g = pl.ds(begin, end - begin)
        near.append(
            (
                exchange(along_y, raw.at[0, core, x, y, g], lambda d, g=g: raw.at[0, core, x, wrap(y + d), g]),
                exchange(along_x, raw.at[1, core, x, y, g], lambda d, g=g: raw.at[1, core, wrap(x + d), y, g]),
            )
        )
    for (begin, end), (wait_y, wait_x) in zip(ZGROUPS, near):
        g = pl.ds(begin, end - begin)
        wait_y()
        wait_first = exchange(along_x, raw.at[0, core, x, :, g], lambda d, g=g: raw.at[0, core, wrap(x + d), :, g])
        wait_x()
        wait_second = exchange(along_y, raw.at[1, core, :, y, g], lambda d, g=g: raw.at[1, core, :, wrap(y + d), g])
        far.append((wait_first, wait_second))
    for (begin, end), waits in zip(ZGROUPS, far):
        g = pl.ds(begin, end - begin)
        for wait in waits:
            wait()
        slot = links.slot()
        links.send(raw.at[:, core, :, :, g], slot, mate)
        handed.append(slot)
        squares = settle(raw, vector, z, core, begin, end, squares)
    for (begin, end), slot in zip(ZGROUPS, handed):
        links.arrived(raw.at[:, 1 - core, :, :, pl.ds(begin, end - begin)], slot, mate)
        squares = settle(raw, vector, z, 1 - core, begin, end, squares)
    return squares


def settle(raw, vector, z, core, begin, end, squares):
    def body(x, squares):
        for h in range(2):
            for y_lo in range(2):
                block = (x * 4 + y_lo * 2 + core) * BLK + h * 2
                for k in range(begin, end):
                    origin = lax.rem(z + (OFFSETS[k] + NZ), NZ)
                    low = raw[h, core, x, y_lo, k].astype(F32)
                    high = raw[h, core, x, y_lo + 2, k].astype(F32)
                    squares = squares + (low[:ROWS] * low[:ROWS] + low[ROWS:] * low[ROWS:])
                    squares = squares + (high[:ROWS] * high[:ROWS] + high[ROWS:] * high[ROWS:])
                    vector[block, origin] = jnp.concatenate([low[:ROWS], high[:ROWS]], axis=0).astype(BF16)
                    vector[block + 1, origin] = jnp.concatenate([low[ROWS:], high[ROWS:]], axis=0).astype(BF16)
        return squares

    return lax.fori_loop(0, NX, body, squares)


def along_z(links, mine, place, at):
    x, y, z, core = at
    slots = [links.slot() for _ in OFFSETS]
    for k in (7, 5, 6, 3, 4, 1, 2):
        links.send(mine, slots[k], device_of(x, y, lax.rem(z - OFFSETS[k] + NZ, NZ), core), place(k))

    def wait(k):
        if k:
            origin = lax.rem(z + (OFFSETS[k] + NZ), NZ)
            links.arrived(place(k), slots[k], device_of(x, y, origin, core))

    return wait


def spread(links, total, out, back, me, at_term):
    for h in range(2):
        rows = [total[h * 2 + k].reshape(N_TERM, ROWS, TILE) for k in range(2)]
        both = jnp.stack(rows, axis=1).reshape(N_TERM, 2 * ROWS, TILE).astype(BF16)
        out[:, h] = both
    slots = [links.slot() for _ in range(1, N_TERM)]
    for d in range(1, N_TERM):
        peer = lax.rem(me + d, N_TERM)
        links.send(out.at[peer], slots[d - 1], at_term(peer), back.at[d])
    return slots


def merge(links, slots, out, back, me, at_term):
    acc = out[me].astype(F32)
    for d in range(1, N_TERM):
        peer = lax.rem(me - d + N_TERM, N_TERM)
        links.arrived(back.at[d], slots[d - 1], at_term(peer))
        acc = acc + back[d].astype(F32)
    return acc.reshape(BLK, ROWS, TILE)


def everyone(links, mine, back, here, n, at):
    slots = [links.slot() for _ in range(1, n)]
    for d in range(1, n):
        links.send(mine, slots[d - 1], at(lax.rem(here + d, n)), back.at[d])

    def wait():
        acc = mine[...]
        for d in range(1, n):
            links.arrived(back.at[d], slots[d - 1], at(lax.rem(here - d + n, n)))
            acc = acc + back[d]
        return acc

    return wait


def kernel(
    psi_hbm,
    diag_hbm,
    shape,
    env_left,
    env_right,
    source_hbm,
    target_hbm,
    left_hbm,
    right_hbm,
    count,
    sigma_one,
    sigma_two,
    psi,
    diag_rows,
    source,
    target,
    left,
    right,
    raw_one,
    raw_two,
    rows_f32,
    vector,
    lefts,
    rights,
    prefix,
    total,
    out_one,
    out_two,
    back_one,
    back_two,
    part,
    part_sector,
    part_term,
    steps_v,
    last_v,
    steps_s,
    last_s,
    local_sem,
    send_sem,
    recv_sem,
):
    term, sector = lax.axis_index("term"), lax.axis_index("sector")
    z, y_hi = lax.div(term, 2), lax.rem(term, 2)
    x, y_lo, core = lax.div(sector, 4), lax.rem(lax.div(sector, 2), 2), lax.rem(sector, 2)
    y = y_hi * 2 + y_lo
    at = (x, y, z, core)

    def at_term(t):
        return (t, sector)

    def at_sector(s):
        return (term, s)

    fetches = [
        pltpu.make_async_copy(here, there, local_sem.at[i])
        for i, (here, there) in enumerate(
            (
                (psi_hbm, psi),
                (diag_hbm, diag_rows),
                (source_hbm, source),
                (target_hbm, target),
                (left_hbm, left),
                (right_hbm, right),
                (env_left.at[0, 0], lefts),
                (env_right.at[0, 0], rights),
            )
        )
    ]
    for fetch in fetches:
        fetch.start()

    barrier = pltpu.get_barrier_semaphore()
    greeted = [at_term(lax.rem(term + d, N_TERM)) for d in range(1, N_TERM)]
    greeted += [at_sector(lax.rem(sector + d, N_SECTOR)) for d in range(1, N_SECTOR)]
    greeted += [(z * 2 + 1 - y_hi, x * 4 + (1 - y_lo) * 2 + core)]
    for device in greeted:
        pl.semaphore_signal(barrier, inc=1, device_id=device, device_id_type=MESH)

    row = lax.broadcasted_iota(I32, (ROWS, TILE), 0) + term * ROWS
    col = lax.broadcasted_iota(I32, (ROWS, TILE), 1)
    inside = [(row < shape[0, b]) & (col < shape[1, b]) for b in range(BLK)]
    prefix[PAIRS] = jnp.zeros((TILE, TILE), BF16)
    for fetch in fetches[:2]:
        fetch.wait()
    diag = diag_rows[...].reshape(BLK, ROWS, TILE)
    given = [psi[h].astype(F32).reshape(2, ROWS, TILE) for h in range(2)]
    start = [jnp.where(inside[b], given[b // 2][b % 2], 0.0) for b in range(BLK)]
    for h in range(2):
        raw_one[h, core, x, y, 0] = jnp.concatenate(start[h * 2 : h * 2 + 2], axis=0).astype(BF16)

    links = Links(send_sem, recv_sem)
    pl.semaphore_wait(barrier, len(greeted))
    arrived = along_z(links, raw_one.at[:, core, x, y, 0], lambda k: raw_one.at[:, core, x, y, k], at)

    for fetch in fetches[2:6]:
        fetch.wait()
    schedule(source[0], target[0], left[0], right[0], count[0, 0], steps_v, last_v)
    copies = [
        pltpu.make_async_copy(steps_v, steps_s, local_sem.at[8]),
        pltpu.make_async_copy(last_v, last_s, local_sem.at[9]),
    ]
    for copy in copies:
        copy.start()

    start_squares = jnp.sum(gather(links, raw_one, vector, at, arrived), keepdims=True)
    for copy in copies + fetches[6:]:
        copy.wait()
    contract(steps_s, last_s, vector, lefts, rights, prefix, total)

    overlap = jnp.zeros((ROWS, TILE), F32)
    for b in range(BLK):
        overlap = overlap + start[b] * start[b] * diag[b]
        tile = vector[sector * BLK + b].astype(F32).reshape(N_TERM, ROWS, TILE)
        overlap = overlap + jnp.sum(tile * total[b].reshape(N_TERM, ROWS, TILE), axis=0)
    part[0] = overlap
    sector_sum = everyone(links, part.at[0], part_sector, sector, N_SECTOR, at_sector)
    slots = spread(links, total, out_one, back_one, term, at_term)
    part[1] = sector_sum()
    term_sum = everyone(links, part.at[1], part_term, term, N_TERM, at_term)
    coupled = merge(links, slots, out_one, back_one, term, at_term)
    sigma = [jnp.where(inside[b], diag[b] * start[b] + coupled[b], 0.0) for b in range(BLK)]
    for b in range(BLK):
        rows_f32[0, b] = sigma[b]
    arrived_f32 = along_z(links, rows_f32.at[0], lambda k: rows_f32.at[k], at)
    for b in range(BLK):
        sigma_one[b] = sigma[b]
    rayleigh = jnp.sum(term_sum(), keepdims=True) / start_squares

    def residual_here(k):
        arrived_f32(k)
        for h in range(2):
            before = raw_one[h, core, x, y, k].astype(F32)
            after = rows_f32[k, h * 2 : h * 2 + 2].reshape(2 * ROWS, TILE)
            raw_two[h, core, x, y, k] = (after - rayleigh * before).astype(BF16)

    squares = jnp.sum(gather(links, raw_two, vector, at, residual_here), keepdims=True)
    scale = lax.rsqrt(squares / float(NBLK * TILE * TILE) + 1e-06)
    contract(steps_s, last_s, vector, lefts, rights, prefix, total)
    slots = spread(links, total, out_two, back_two, term, at_term)
    coupled = merge(links, slots, out_two, back_two, term, at_term)
    for b in range(BLK):
        second = raw_two[b // 2, core, x, y, 0].astype(F32)[(b % 2) * ROWS : (b % 2 + 1) * ROWS]
        sigma_two[b] = jnp.where(inside[b], (diag[b] * second + coupled[b]) * scale, 0.0)
    links.drain()


def body(psi, diag_energy, block_shape, *rest):
    vmem = pl.BlockSpec(memory_space=pltpu.VMEM)
    smem = pl.BlockSpec(memory_space=pltpu.SMEM)
    hbm = pl.BlockSpec(memory_space=pltpu.HBM)
    out = jax.ShapeDtypeStruct((BLK, ROWS, TILE), F32)
    raw = pltpu.VMEM((2, NCORE, NX, NY, NZ, 2 * ROWS, TILE), BF16)
    rows = pltpu.VMEM((N_TERM, 2, 2 * ROWS, TILE), BF16)
    slots = pltpu.VMEM((1, 1, PAIRS), I32)
    return pl.pallas_call(
        kernel,
        out_shape=(out, out),
        in_specs=[hbm, hbm, smem, hbm, hbm, hbm, hbm, hbm, hbm, smem],
        out_specs=(vmem, vmem),
        scratch_shapes=[
            pltpu.VMEM((2, 2 * ROWS, TILE), BF16),
            pltpu.VMEM((BLK * ROWS, TILE), F32),
            slots,
            slots,
            slots,
            slots,
            raw,
            raw,
            pltpu.VMEM((NZ, BLK, ROWS, TILE), F32),
            pltpu.VMEM((NBLK, NZ, 2 * ROWS, TILE), BF16),
            pltpu.VMEM((ENV, TILE, TILE), BF16),
            pltpu.VMEM((ENV, TILE, TILE), BF16),
            pltpu.VMEM((PAIRS + 1, TILE, TILE), BF16),
            pltpu.VMEM((BLK, TILE, TILE), F32),
            rows,
            rows,
            rows,
            rows,
            pltpu.VMEM((2, ROWS, TILE), F32),
            pltpu.VMEM((N_SECTOR, ROWS, TILE), F32),
            pltpu.VMEM((N_TERM, ROWS, TILE), F32),
            pltpu.VMEM((8, PAIRS), I32),
            pltpu.VMEM((8, TILE), I32),
            pltpu.SMEM((8, PAIRS), I32),
            pltpu.SMEM((8, TILE), I32),
            pltpu.SemaphoreType.DMA((10,)),
            pltpu.SemaphoreType.DMA((N_SEND,)),
            pltpu.SemaphoreType.DMA((N_SEND,)),
        ],
        compiler_params=pltpu.CompilerParams(
            collective_id=0, has_side_effects=True, vmem_limit_bytes=60 * 2**20
        ),
        name="two_products",
    )(psi.reshape(2, 2 * ROWS, TILE), diag_energy.reshape(BLK * ROWS, TILE), block_shape.T, *rest)


def solution(mesh):
    placed = (
        P("sector", "term", None),
        P("sector", "term", None),
        P("sector", None),
        P("term", "sector", None, None, None),
        P("term", "sector", None, None, None),
        P("term", "sector", None),
        P("term", "sector", None),
        P("term", "sector", None),
        P("term", "sector", None),
        P("term", "sector"),
    )
    return jax.shard_map(
        body,
        mesh=mesh,
        in_specs=placed,
        out_specs=(P("sector", "term", None), P("sector", "term", None)),
        check_vma=False,
    )
```

```python
import functools

import jax
import jax.numpy as jnp
from jax import lax
from jax.experimental import pallas as pl
from jax.experimental.pallas import tpu as pltpu
from jax.sharding import PartitionSpec as P

F32 = jnp.float32
BF16 = jnp.bfloat16
I32 = jnp.int32
MESH = pl.DeviceIdType.MESH

TILE = 128
PAIRS = 384
ENV = 32
BLK = 4
ROWS = 8
NX, NY, NZ, NCORE = 4, 4, 8, 2
N_TERM, N_SECTOR = 16, 16
NBLK = N_SECTOR * BLK
GROUPS = ENV * BLK
UNROLL = 96
N_SEND = 64
OFFSETS = (0, 1, -1, 2, -2, 3, -3, 4)
ZGROUPS = ((0, 1), (1, 3), (3, 5), (5, 7), (7, 8))


def order_of(*marks):
    names = {"n": "near", "f": "far", "h": "hand", "t": "take"}
    return tuple((names[mark[0]], int(mark[1:])) for mark in marks)


ENDS = ("h0", "h1", "t0", "h2", "t1", "h3", "t2", "h4", "t3", "t4")
ORDER_ONE = order_of("n0", "n1", "n2", "f0", "n3", "n4", "f1", "f2", "f3", "f4", *ENDS)
ORDER_TWO = order_of("n0", "n1", "n2", "n3", "n4", "f0", "f1", "f2", "f3", "f4", *ENDS)
NT = (((1,), (1,)), ((), ()))


def dot(a, b):
    return jnp.dot(a, b, preferred_element_type=F32)


def as_bf16(flags):
    return flags.astype(F32).astype(BF16)


def schedule(source, target, left, right, count, steps_ref, last_ref):
    slot = lax.broadcasted_iota(I32, (1, PAIRS), 1)
    live = slot < count
    key = jnp.where(live, left * BLK + target, GROUPS)
    member = lax.broadcasted_iota(I32, (GROUPS, PAIRS), 0) == key
    member_f = member.astype(F32)
    member_b = member_f.astype(BF16)
    earlier = as_bf16(
        lax.broadcasted_iota(I32, (PAIRS, PAIRS), 0) < lax.broadcasted_iota(I32, (PAIRS, PAIRS), 1)
    )
    rank = jnp.sum(member_f * dot(member_b, earlier), axis=0, keepdims=True)
    row_g = lax.broadcasted_iota(I32, (GROUPS, GROUPS), 0)
    col_g = lax.broadcasted_iota(I32, (GROUPS, GROUPS), 1)
    size = jnp.broadcast_to(jnp.sum(member_f, axis=1, keepdims=True), (GROUPS, GROUPS))
    high = jnp.floor(size * (1.0 / 16.0))
    low = size - 16.0 * high
    below = as_bf16(col_g < row_g)
    begin = 16.0 * dot(below, high.astype(BF16)) + dot(below, low.astype(BF16))
    begin_of = jnp.sum(member_f * begin[:, :1], axis=0, keepdims=True)
    place = jnp.where(live, (rank + begin_of).astype(I32), -1)
    sent = as_bf16(lax.broadcasted_iota(I32, (PAIRS, PAIRS), 0) == place)
    line = lax.broadcasted_iota(I32, (8, PAIRS), 0)
    table = jnp.where(line == 0, source, jnp.where(line == 1, right, jnp.where(line == 2, key, 0)))
    moved = lax.dot_general(table.astype(F32).astype(BF16), sent, NT, preferred_element_type=F32)
    again = (moved == pltpu.roll(moved, 1, 1)) & (lax.broadcasted_iota(I32, (8, PAIRS), 1) > 0)
    top = jnp.where(line == 0, NBLK - 1, jnp.where(line == 1, ENV - 1, 1))
    steps_ref[...] = jnp.clip(jnp.where(line == 2, again.astype(I32), moved.astype(I32)), 0, top)
    size = lax.dot_general(jnp.ones((8, PAIRS), BF16), member_b, NT, preferred_element_type=F32)
    high = jnp.floor(size * (1.0 / 16.0))
    low = size - 16.0 * high
    above = as_bf16(row_g < col_g)
    begin = 16.0 * dot(high.astype(BF16), above) + dot(low.astype(BF16), above)
    ends = (begin + size).astype(I32) - 1
    last_ref[...] = jnp.where(size > 0.5, jnp.clip(ends, 0, PAIRS - 1), PAIRS)


def contract(steps, last, vector, lefts, rights, prefix, total):
    def step_body(turn, running):
        for u in range(UNROLL):
            k = turn * UNROLL + u
            keep = steps[2, k].astype(F32)
            tile = vector[steps[0, k]].reshape(TILE, TILE)
            running = running * keep + dot(tile, rights[steps[1, k]])
            prefix[k] = running.astype(BF16)
        return running

    lax.fori_loop(0, PAIRS // UNROLL, step_body, jnp.zeros((TILE, TILE), F32))
    for half in range(2):
        running = jnp.zeros((TILE, 2 * TILE), F32)
        for l in range(0, ENV, 2):
            tiles = jnp.concatenate([lefts[l], lefts[l + 1]], axis=1)
            sums = [
                jnp.concatenate([prefix[last[0, (l + dl) * BLK + half * 2 + db]] for db in range(2)], axis=1)
                for dl in range(2)
            ]
            running = running + dot(tiles, jnp.concatenate(sums, axis=0))
        total[half * 2] = running[:, :TILE]
        total[half * 2 + 1] = running[:, TILE:]


def device_of(x, y, z, core):
    return (z * 2 + lax.div(y, 2), x * 4 + lax.rem(y, 2) * 2 + core)


class Links:
    def __init__(self, send_sem, recv_sem, device):
        self.send_sem, self.recv_sem, self.device = send_sem, recv_sem, device
        self.used = 0
        self.pending = []

    def slot(self, whole):
        self.used += 1
        self.pending.append((whole, self.used - 1))
        return self.used - 1

    def copy(self, ref, slot, device, dst=None):
        return pltpu.make_async_remote_copy(
            src_ref=ref,
            dst_ref=ref if dst is None else dst,
            send_sem=self.send_sem.at[slot],
            recv_sem=self.recv_sem.at[slot],
            device_id=device,
            device_id_type=MESH,
        )

    def send(self, ref, slot, device, dst=None):
        self.copy(ref, slot, device, dst).start()

    def arrived(self, whole, slot):
        self.copy(whole, slot, self.device).wait_recv()

    def drain(self, pending=None):
        for whole, slot in list(self.pending) if pending is None else pending:
            self.copy(whole, slot, self.device).wait_send()
            self.pending.remove((whole, slot))


def gather(links, raw, vector, at, ready, order):
    x, y, z, core = at
    mate = device_of(x, y, z, 1 - core)
    squares = jnp.zeros((ROWS, TILE), F32)

    def wrap(i):
        return lax.rem(i, 4)

    def along_x(step):
        return device_of(wrap(x + step), y, z, core)

    def along_y(step):
        return device_of(x, wrap(y + step), z, core)

    def exchange(along, mine, three):
        slot = links.slot(three)
        for d in (2, 1, 3):
            links.send(mine, slot, along(d))
        return lambda: links.arrived(three, slot)

    others = pl.ds(0, 3)
    state = [None] * len(ZGROUPS)
    for event, i in order:
        begin, end = ZGROUPS[i]
        g = pl.ds(begin, end - begin)
        if event == "near":
            ready(begin, end)
            state[i] = (
                exchange(along_y, raw.at[0, core, x, y, g], raw.at[0, core, x, others, g]),
                exchange(along_x, raw.at[1, core, x, y, g], raw.at[1, core, others, y, g]),
            )
        elif event == "far":
            wait_y, wait_x = state[i]
            wait_y()
            first = exchange(along_x, raw.at[0, core, x, :, g], raw.at[0, core, others, :, g])
            wait_x()
            second = exchange(along_y, raw.at[1, core, :, y, g], raw.at[1, core, :, others, g])
            state[i] = (first, second)
        elif event == "hand":
            for wait in state[i]:
                wait()
            here = raw.at[:, core, :, :, g]
            state[i] = links.slot(here)
            links.send(here, state[i], mate)
            squares = settle(raw, vector, z, core, begin, end, squares)
        else:
            links.arrived(raw.at[:, 1 - core, :, :, g], state[i])
            squares = settle(raw, vector, z, 1 - core, begin, end, squares)
    return squares


def settle(raw, vector, z, core, begin, end, squares):
    def body(x, squares):
        for h in range(2):
            for y_lo in range(2):
                block = (x * 4 + y_lo * 2 + core) * BLK + h * 2
                for k in range(begin, end):
                    origin = lax.rem(z + (OFFSETS[k] + NZ), NZ)
                    low = raw[h, core, x, y_lo, k].astype(F32)
                    high = raw[h, core, x, y_lo + 2, k].astype(F32)
                    squares = squares + (low[:ROWS] * low[:ROWS] + low[ROWS:] * low[ROWS:])
                    squares = squares + (high[:ROWS] * high[:ROWS] + high[ROWS:] * high[ROWS:])
                    vector[block, origin] = jnp.concatenate([low[:ROWS], high[:ROWS]], axis=0).astype(BF16)
                    vector[block + 1, origin] = jnp.concatenate([low[ROWS:], high[ROWS:]], axis=0).astype(BF16)
        return squares

    return lax.fori_loop(0, NX, body, squares)


def along_z(links, mine, place, at):
    x, y, z, core = at
    slots = [links.slot(place(pl.ds(max(begin, 1), end - max(begin, 1)))) if end > 1 else None for begin, end in ZGROUPS]
    group = [i for i, (begin, end) in enumerate(ZGROUPS) for _ in range(begin, end)]
    for k in (7, 5, 6, 3, 4, 1, 2):
        to = device_of(x, y, lax.rem(z - OFFSETS[k] + NZ, NZ), core)
        links.send(mine, slots[group[k]], to, place(k))

    def wait(begin, end):
        slot = slots[group[begin]]
        if slot is not None:
            begin = max(begin, 1)
            links.arrived(place(pl.ds(begin, end - begin)), slot)

    return wait


def spread(links, total, out, back, me, at_term):
    for h in range(2):
        rows = [total[h * 2 + k].reshape(N_TERM, ROWS, TILE) for k in range(2)]
        both = jnp.stack(rows, axis=1).reshape(N_TERM, 2 * ROWS, TILE).astype(BF16)
        out[:, h] = both
    peers = pl.ds(1, N_TERM - 1)
    slot = links.slot(back.at[peers])
    for d in sorted(range(1, N_TERM), key=lambda d: abs(d - N_TERM // 2)):
        peer = lax.rem(me + d, N_TERM)
        links.send(out.at[peer], slot, at_term(peer), back.at[d])

    def wait():
        acc = out[me].astype(F32)
        links.arrived(back.at[peers], slot)
        return (acc + jnp.sum(back[peers].astype(F32), axis=0)).reshape(BLK, ROWS, TILE)

    return wait


def everyone(links, mine, back, here, n, at):
    peers = pl.ds(1, n - 1)
    slot = links.slot(back.at[peers])
    for d in sorted(range(1, n), key=lambda d: abs(d - n // 2)):
        links.send(mine, slot, at(lax.rem(here + d, n)), back.at[d])

    def wait():
        acc = mine[...]
        links.arrived(back.at[peers], slot)
        return acc + jnp.sum(back[peers], axis=0)

    return wait


def kernel(
    psi_hbm,
    diag_hbm,
    shape,
    env_left,
    env_right,
    source_hbm,
    target_hbm,
    left_hbm,
    right_hbm,
    count,
    sigma_one,
    sigma_two,
    psi,
    diag_rows,
    source,
    target,
    left,
    right,
    raw_one,
    raw_two,
    rows_f32,
    vector,
    lefts,
    rights,
    prefix,
    total,
    out_one,
    out_two,
    back_one,
    back_two,
    part,
    part_sector,
    part_term,
    steps_v,
    last_v,
    steps_s,
    last_s,
    local_sem,
    send_sem,
    recv_sem,
):
    term, sector = lax.axis_index("term"), lax.axis_index("sector")
    z, y_hi = lax.div(term, 2), lax.rem(term, 2)
    x, y_lo, core = lax.div(sector, 4), lax.rem(lax.div(sector, 2), 2), lax.rem(sector, 2)
    y = y_hi * 2 + y_lo
    at = (x, y, z, core)

    def at_term(t):
        return (t, sector)

    def at_sector(s):
        return (term, s)

    fetches = [
        pltpu.make_async_copy(here, there, local_sem.at[i])
        for i, (here, there) in enumerate(
            (
                (psi_hbm, psi),
                (diag_hbm, diag_rows),
                (source_hbm, source),
                (target_hbm, target),
                (left_hbm, left),
                (right_hbm, right),
                (env_left.at[0, 0], lefts),
                (env_right.at[0, 0], rights),
            )
        )
    ]
    for fetch in fetches:
        fetch.start()

    barrier = pltpu.get_barrier_semaphore()
    greeted = [at_term(lax.rem(term + d, N_TERM)) for d in range(1, N_TERM)]
    greeted += [at_sector(lax.rem(sector + d, N_SECTOR)) for d in range(1, N_SECTOR)]
    chip = lax.div(sector, 2)
    greeted += [(z * 2 + 1 - y_hi, lax.rem(chip + d, N_SECTOR // 2) * 2 + core) for d in range(1, N_SECTOR // 2)]
    for device in greeted:
        pl.semaphore_signal(barrier, inc=1, device_id=device, device_id_type=MESH)

    row = lax.broadcasted_iota(I32, (ROWS, TILE), 0) + term * ROWS
    col = lax.broadcasted_iota(I32, (ROWS, TILE), 1)
    inside = [(row < shape[0, b]) & (col < shape[1, b]) for b in range(BLK)]
    prefix[PAIRS] = jnp.zeros((TILE, TILE), BF16)
    for fetch in fetches[:2]:
        fetch.wait()
    diag = diag_rows[...].reshape(BLK, ROWS, TILE)
    given = [psi[h].astype(F32).reshape(2, ROWS, TILE) for h in range(2)]
    start = [jnp.where(inside[b], given[b // 2][b % 2], 0.0) for b in range(BLK)]
    for h in range(2):
        raw_one[h, core, x, y, 0] = jnp.concatenate(start[h * 2 : h * 2 + 2], axis=0).astype(BF16)

    links = Links(send_sem, recv_sem, device_of(x, y, z, 1 - core))
    pl.semaphore_wait(barrier, len(greeted))
    arrived = along_z(links, raw_one.at[:, core, x, y, 0], lambda k: raw_one.at[:, core, x, y, k], at)

    for fetch in fetches[2:6]:
        fetch.wait()
    schedule(source[0], target[0], left[0], right[0], count[0, 0], steps_v, last_v)
    copies = [
        pltpu.make_async_copy(steps_v, steps_s, local_sem.at[8]),
        pltpu.make_async_copy(last_v, last_s, local_sem.at[9]),
    ]
    for copy in copies:
        copy.start()

    start_squares = jnp.sum(gather(links, raw_one, vector, at, arrived, ORDER_ONE), keepdims=True)
    for copy in copies + fetches[6:]:
        copy.wait()
    contract(steps_s, last_s, vector, lefts, rights, prefix, total)

    overlap = jnp.zeros((ROWS, TILE), F32)
    for b in range(BLK):
        overlap = overlap + start[b] * start[b] * diag[b]
        tile = vector[sector * BLK + b].astype(F32).reshape(N_TERM, ROWS, TILE)
        overlap = overlap + jnp.sum(tile * total[b].reshape(N_TERM, ROWS, TILE), axis=0)
    part[0] = overlap
    gathered = list(links.pending)
    sector_sum = everyone(links, part.at[0], part_sector, sector, N_SECTOR, at_sector)
    rows_sum = spread(links, total, out_one, back_one, term, at_term)
    part[1] = sector_sum()
    term_sum = everyone(links, part.at[1], part_term, term, N_TERM, at_term)
    links.drain(gathered)
    coupled = rows_sum()
    sigma = [jnp.where(inside[b], diag[b] * start[b] + coupled[b], 0.0) for b in range(BLK)]
    for b in range(BLK):
        rows_f32[0, b] = sigma[b]
    arrived_f32 = along_z(links, rows_f32.at[0], lambda k: rows_f32.at[k], at)
    for b in range(BLK):
        sigma_one[b] = sigma[b]
    rayleigh = jnp.sum(term_sum(), keepdims=True) / start_squares

    def residual_here(begin, end):
        arrived_f32(begin, end)
        for k in range(begin, end):
            for h in range(2):
                before = raw_one[h, core, x, y, k].astype(F32)
                after = rows_f32[k, h * 2 : h * 2 + 2].reshape(2 * ROWS, TILE)
                raw_two[h, core, x, y, k] = (after - rayleigh * before).astype(BF16)

    squares = jnp.sum(gather(links, raw_two, vector, at, residual_here, ORDER_TWO), keepdims=True)
    scale = lax.rsqrt(squares / float(NBLK * TILE * TILE) + 1e-06)
    contract(steps_s, last_s, vector, lefts, rights, prefix, total)
    gathered = list(links.pending)
    rows_sum = spread(links, total, out_two, back_two, term, at_term)
    links.drain(gathered)
    coupled = rows_sum()
    for b in range(BLK):
        second = raw_two[b // 2, core, x, y, 0].astype(F32)[(b % 2) * ROWS : (b % 2 + 1) * ROWS]
        sigma_two[b] = jnp.where(inside[b], (diag[b] * second + coupled[b]) * scale, 0.0)
    links.drain()


def keep_kernel(one, two, one_out, two_out, sem):
    copies = [
        pltpu.make_async_copy(one, one_out, sem.at[0]),
        pltpu.make_async_copy(two, two_out, sem.at[1]),
    ]
    for copy in copies:
        copy.start()
    for copy in copies:
        copy.wait()


def body(psi, diag_energy, block_shape, *rest):
    vmem = pl.BlockSpec(memory_space=pltpu.VMEM)
    smem = pl.BlockSpec(memory_space=pltpu.SMEM)
    hbm = pl.BlockSpec(memory_space=pltpu.HBM)
    out = jax.ShapeDtypeStruct((BLK, ROWS, TILE), F32)
    raw = pltpu.VMEM((2, NCORE, NX, NY, NZ, 2 * ROWS, TILE), BF16)
    rows = pltpu.VMEM((N_TERM, 2, 2 * ROWS, TILE), BF16)
    slots = pltpu.VMEM((1, 1, PAIRS), I32)
    sums = pl.pallas_call(
        kernel,
        out_shape=(out, out),
        in_specs=[hbm, hbm, smem, hbm, hbm, hbm, hbm, hbm, hbm, smem],
        out_specs=(vmem, vmem),
        scratch_shapes=[
            pltpu.VMEM((2, 2 * ROWS, TILE), BF16),
            pltpu.VMEM((BLK * ROWS, TILE), F32),
            slots,
            slots,
            slots,
            slots,
            raw,
            raw,
            pltpu.VMEM((NZ, BLK, ROWS, TILE), F32),
            pltpu.VMEM((NBLK, NZ, 2 * ROWS, TILE), BF16),
            pltpu.VMEM((ENV, TILE, TILE), BF16),
            pltpu.VMEM((ENV, TILE, TILE), BF16),
            pltpu.VMEM((PAIRS + 1, TILE, TILE), BF16),
            pltpu.VMEM((BLK, TILE, TILE), F32),
            rows,
            rows,
            rows,
            rows,
            pltpu.VMEM((2, ROWS, TILE), F32),
            pltpu.VMEM((N_SECTOR, ROWS, TILE), F32),
            pltpu.VMEM((N_TERM, ROWS, TILE), F32),
            pltpu.VMEM((8, PAIRS), I32),
            pltpu.VMEM((8, TILE), I32),
            pltpu.SMEM((8, PAIRS), I32),
            pltpu.SMEM((8, TILE), I32),
            pltpu.SemaphoreType.DMA((10,)),
            pltpu.SemaphoreType.DMA((N_SEND,)),
            pltpu.SemaphoreType.DMA((N_SEND,)),
        ],
        compiler_params=pltpu.CompilerParams(
            collective_id=0, has_side_effects=True, vmem_limit_bytes=60 * 2**20
        ),
        name="two_products",
    )(psi.reshape(2, 2 * ROWS, TILE), diag_energy.reshape(BLK * ROWS, TILE), block_shape.T, *rest)
    return pl.pallas_call(
        keep_kernel,
        out_shape=(out, out),
        in_specs=[hbm, hbm],
        out_specs=(hbm, hbm),
        scratch_shapes=[pltpu.SemaphoreType.DMA((2,))],
        name="keep",
    )(*sums)


def solution(mesh):
    placed = (
        P("sector", "term", None),
        P("sector", "term", None),
        P("sector", None),
        P("term", "sector", None, None, None),
        P("term", "sector", None, None, None),
        P("term", "sector", None),
        P("term", "sector", None),
        P("term", "sector", None),
        P("term", "sector", None),
        P("term", "sector"),
    )
    return jax.shard_map(
        body,
        mesh=mesh,
        in_specs=placed,
        out_specs=(P("sector", "term", None), P("sector", "term", None)),
        check_vma=False,
    )
```

```python
import functools

import jax
import jax.numpy as jnp
from jax import lax
from jax.experimental import pallas as pl
from jax.experimental.pallas import tpu as pltpu
from jax.sharding import PartitionSpec as P

F32 = jnp.float32
BF16 = jnp.bfloat16
I32 = jnp.int32
MESH = pl.DeviceIdType.MESH

TILE = 128
PAIRS = 384
ENV = 32
BLK = 4
ROWS = 8
NX, NY, NZ, NCORE = 4, 4, 8, 2
N_TERM, N_SECTOR = 16, 16
NBLK = N_SECTOR * BLK
GROUPS = ENV * BLK
UNROLL = 192
N_SEND = 64
OFFSETS = (0, 1, -1, 2, -2, 3, -3, 4)
ZGROUPS = ((0, 1), (1, 3), (3, 5), (5, 7), (7, 8))


def order_of(*marks):
    names = {"n": "near", "f": "far", "h": "hand", "t": "take", "a": "aside"}
    return tuple((names[mark[0]], int(mark[1:])) for mark in marks)


ENDS = ("h0", "h1", "t0", "h2", "t1", "h3", "t2", "h4", "t3", "t4")
ORDER_ONE = order_of("n0", "a0", "n1", "n2", "f0", "n3", "n4", "f1", "f2", "f3", "f4", *ENDS)
ORDER_TWO = order_of("n0", "n1", "n2", "n3", "n4", "f0", "f1", "f2", "f3", "f4", *ENDS)
NT = (((1,), (1,)), ((), ()))


def dot(a, b):
    return jnp.dot(a, b, preferred_element_type=F32)


def as_bf16(flags):
    return flags.astype(F32).astype(BF16)


def schedule(source, target, left, right, count, steps_ref, last_ref):
    slot = lax.broadcasted_iota(I32, (1, PAIRS), 1)
    live = slot < count
    key = jnp.where(live, left * BLK + target, GROUPS)
    member = lax.broadcasted_iota(I32, (GROUPS, PAIRS), 0) == key
    member_f = member.astype(F32)
    member_b = member_f.astype(BF16)
    earlier = as_bf16(
        lax.broadcasted_iota(I32, (PAIRS, PAIRS), 0) < lax.broadcasted_iota(I32, (PAIRS, PAIRS), 1)
    )
    rank = jnp.sum(member_f * dot(member_b, earlier), axis=0, keepdims=True)
    row_g = lax.broadcasted_iota(I32, (GROUPS, GROUPS), 0)
    col_g = lax.broadcasted_iota(I32, (GROUPS, GROUPS), 1)
    size = jnp.broadcast_to(jnp.sum(member_f, axis=1, keepdims=True), (GROUPS, GROUPS))
    high = jnp.floor(size * (1.0 / 16.0))
    low = size - 16.0 * high
    below = as_bf16(col_g < row_g)
    begin = 16.0 * dot(below, high.astype(BF16)) + dot(below, low.astype(BF16))
    begin_of = jnp.sum(member_f * begin[:, :1], axis=0, keepdims=True)
    place = jnp.where(live, (rank + begin_of).astype(I32), -1)
    sent = as_bf16(lax.broadcasted_iota(I32, (PAIRS, PAIRS), 0) == place)
    line = lax.broadcasted_iota(I32, (8, PAIRS), 0)
    table = jnp.where(line == 0, source, jnp.where(line == 1, right, jnp.where(line == 2, key, 0)))
    moved = lax.dot_general(table.astype(F32).astype(BF16), sent, NT, preferred_element_type=F32)
    again = (moved == pltpu.roll(moved, 1, 1)) & (lax.broadcasted_iota(I32, (8, PAIRS), 1) > 0)
    top = jnp.where(line == 0, NBLK - 1, jnp.where(line == 1, ENV - 1, 1))
    steps_ref[...] = jnp.clip(jnp.where(line == 2, again.astype(I32), moved.astype(I32)), 0, top)
    size = lax.dot_general(jnp.ones((8, PAIRS), BF16), member_b, NT, preferred_element_type=F32)
    high = jnp.floor(size * (1.0 / 16.0))
    low = size - 16.0 * high
    above = as_bf16(row_g < col_g)
    begin = 16.0 * dot(high.astype(BF16), above) + dot(low.astype(BF16), above)
    ends = (begin + size).astype(I32) - 1
    last_ref[...] = jnp.where(size > 0.5, jnp.clip(ends, 0, PAIRS - 1), PAIRS)


def contract(steps, last, vector, lefts, rights, prefix, total):
    def step_body(turn, running):
        for u in range(UNROLL):
            k = turn * UNROLL + u
            keep = steps[2, k].astype(F32)
            tile = vector[steps[0, k]].reshape(TILE, TILE)
            running = running * keep + dot(tile, rights[steps[1, k]])
            prefix[k] = running.astype(BF16)
        return running

    lax.fori_loop(0, PAIRS // UNROLL, step_body, jnp.zeros((TILE, TILE), F32))
    for half in range(2):
        running = jnp.zeros((TILE, 2 * TILE), F32)
        for l in range(0, ENV, 2):
            tiles = jnp.concatenate([lefts[l], lefts[l + 1]], axis=1)
            sums = [
                jnp.concatenate([prefix[last[0, (l + dl) * BLK + half * 2 + db]] for db in range(2)], axis=1)
                for dl in range(2)
            ]
            running = running + dot(tiles, jnp.concatenate(sums, axis=0))
        total[half * 2] = running[:, :TILE]
        total[half * 2 + 1] = running[:, TILE:]


def device_of(x, y, z, core):
    return (z * 2 + lax.div(y, 2), x * 4 + lax.rem(y, 2) * 2 + core)


class Links:
    def __init__(self, send_sem, recv_sem, device):
        self.send_sem, self.recv_sem, self.device = send_sem, recv_sem, device
        self.used = 0
        self.pending = []

    def slot(self, whole):
        self.used += 1
        self.pending.append((whole, self.used - 1))
        return self.used - 1

    def copy(self, ref, slot, device, dst=None):
        return pltpu.make_async_remote_copy(
            src_ref=ref,
            dst_ref=ref if dst is None else dst,
            send_sem=self.send_sem.at[slot],
            recv_sem=self.recv_sem.at[slot],
            device_id=device,
            device_id_type=MESH,
        )

    def send(self, ref, slot, device, dst=None):
        self.copy(ref, slot, device, dst).start()

    def arrived(self, whole, slot):
        self.copy(whole, slot, self.device).wait_recv()

    def drain(self, pending=None):
        for whole, slot in list(self.pending) if pending is None else pending:
            self.copy(whole, slot, self.device).wait_send()
            self.pending.remove((whole, slot))


def gather(links, raw, vector, at, ready, order, aside=None):
    x, y, z, core = at
    mate = device_of(x, y, z, 1 - core)
    squares = jnp.zeros((ROWS, TILE), F32)

    def wrap(i):
        return lax.rem(i, 4)

    def along_x(step):
        return device_of(wrap(x + step), y, z, core)

    def along_y(step):
        return device_of(x, wrap(y + step), z, core)

    def exchange(along, mine, three):
        slot = links.slot(three)
        for d in (2, 1, 3):
            links.send(mine, slot, along(d))
        return lambda: links.arrived(three, slot)

    others = pl.ds(0, 3)
    state = [None] * len(ZGROUPS)
    for event, i in order:
        begin, end = ZGROUPS[i]
        g = pl.ds(begin, end - begin)
        if event == "aside":
            aside()
        elif event == "near":
            ready(begin, end)
            state[i] = (
                exchange(along_y, raw.at[0, core, x, y, g], raw.at[0, core, x, others, g]),
                exchange(along_x, raw.at[1, core, x, y, g], raw.at[1, core, others, y, g]),
            )
        elif event == "far":
            wait_y, wait_x = state[i]
            wait_y()
            first = exchange(along_x, raw.at[0, core, x, :, g], raw.at[0, core, others, :, g])
            wait_x()
            second = exchange(along_y, raw.at[1, core, :, y, g], raw.at[1, core, :, others, g])
            state[i] = (first, second)
        elif event == "hand":
            for wait in state[i]:
                wait()
            here = raw.at[:, core, :, :, g]
            state[i] = links.slot(here)
            links.send(here, state[i], mate)
            squares = settle(raw, vector, z, core, begin, end, squares)
        else:
            links.arrived(raw.at[:, 1 - core, :, :, g], state[i])
            squares = settle(raw, vector, z, 1 - core, begin, end, squares)
    return squares


def settle(raw, vector, z, core, begin, end, squares):
    def body(x, squares):
        for h in range(2):
            for y_lo in range(2):
                block = (x * 4 + y_lo * 2 + core) * BLK + h * 2
                for k in range(begin, end):
                    origin = lax.rem(z + (OFFSETS[k] + NZ), NZ)
                    low = raw[h, core, x, y_lo, k].astype(F32)
                    high = raw[h, core, x, y_lo + 2, k].astype(F32)
                    squares = squares + (low[:ROWS] * low[:ROWS] + low[ROWS:] * low[ROWS:])
                    squares = squares + (high[:ROWS] * high[:ROWS] + high[ROWS:] * high[ROWS:])
                    vector[block, origin] = jnp.concatenate([low[:ROWS], high[:ROWS]], axis=0).astype(BF16)
                    vector[block + 1, origin] = jnp.concatenate([low[ROWS:], high[ROWS:]], axis=0).astype(BF16)
        return squares

    return lax.fori_loop(0, NX, body, squares)


def along_z(links, mine, place, at):
    x, y, z, core = at
    slots = [links.slot(place(pl.ds(max(begin, 1), end - max(begin, 1)))) if end > 1 else None for begin, end in ZGROUPS]
    group = [i for i, (begin, end) in enumerate(ZGROUPS) for _ in range(begin, end)]
    for k in (7, 5, 6, 3, 4, 1, 2):
        to = device_of(x, y, lax.rem(z - OFFSETS[k] + NZ, NZ), core)
        links.send(mine, slots[group[k]], to, place(k))

    def wait(begin, end):
        slot = slots[group[begin]]
        if slot is not None:
            begin = max(begin, 1)
            links.arrived(place(pl.ds(begin, end - begin)), slot)

    return wait


def spread(links, total, out, back, me, at_term):
    for h in range(2):
        rows = [total[h * 2 + k].reshape(N_TERM, ROWS, TILE) for k in range(2)]
        both = jnp.stack(rows, axis=1).reshape(N_TERM, 2 * ROWS, TILE).astype(BF16)
        out[:, h] = both
    peers = pl.ds(1, N_TERM - 1)
    slot = links.slot(back.at[peers])
    for d in sorted(range(1, N_TERM), key=lambda d: abs(d - N_TERM // 2)):
        peer = lax.rem(me + d, N_TERM)
        links.send(out.at[peer], slot, at_term(peer), back.at[d])

    def wait():
        acc = out[me].astype(F32)
        links.arrived(back.at[peers], slot)
        return (acc + jnp.sum(back[peers].astype(F32), axis=0)).reshape(BLK, ROWS, TILE)

    return wait


def everyone(links, mine, back, here, n, at):
    peers = pl.ds(1, n - 1)
    slot = links.slot(back.at[peers])
    for d in sorted(range(1, n), key=lambda d: abs(d - n // 2)):
        links.send(mine, slot, at(lax.rem(here + d, n)), back.at[d])

    def wait():
        acc = mine[...]
        links.arrived(back.at[peers], slot)
        return acc + jnp.sum(back[peers], axis=0)

    return wait


def kernel(
    psi_hbm,
    diag_hbm,
    shape,
    env_left,
    env_right,
    source_hbm,
    target_hbm,
    left_hbm,
    right_hbm,
    count,
    sigma_one,
    sigma_two,
    psi,
    diag_rows,
    source,
    target,
    left,
    right,
    raw_one,
    raw_two,
    rows_f32,
    vector,
    lefts,
    rights,
    prefix,
    total,
    out_one,
    out_two,
    back_one,
    back_two,
    part,
    part_sector,
    part_term,
    steps_v,
    last_v,
    steps_s,
    last_s,
    local_sem,
    send_sem,
    recv_sem,
):
    term, sector = lax.axis_index("term"), lax.axis_index("sector")
    z, y_hi = lax.div(term, 2), lax.rem(term, 2)
    x, y_lo, core = lax.div(sector, 4), lax.rem(lax.div(sector, 2), 2), lax.rem(sector, 2)
    y = y_hi * 2 + y_lo
    at = (x, y, z, core)

    def at_term(t):
        return (t, sector)

    def at_sector(s):
        return (term, s)

    fetches = [
        pltpu.make_async_copy(here, there, local_sem.at[i])
        for i, (here, there) in enumerate(
            (
                (psi_hbm, psi),
                (diag_hbm, diag_rows),
                (source_hbm, source),
                (target_hbm, target),
                (left_hbm, left),
                (right_hbm, right),
                (env_left.at[0, 0], lefts),
                (env_right.at[0, 0], rights),
            )
        )
    ]
    for fetch in fetches:
        fetch.start()

    barrier = pltpu.get_barrier_semaphore()
    greeted = [at_term(lax.rem(term + d, N_TERM)) for d in range(1, N_TERM)]
    greeted += [at_sector(lax.rem(sector + d, N_SECTOR)) for d in range(1, N_SECTOR)]
    chip = lax.div(sector, 2)
    greeted += [(z * 2 + 1 - y_hi, lax.rem(chip + d, N_SECTOR // 2) * 2 + core) for d in range(1, N_SECTOR // 2)]
    for device in greeted:
        pl.semaphore_signal(barrier, inc=1, device_id=device, device_id_type=MESH)

    row = lax.broadcasted_iota(I32, (ROWS, TILE), 0) + term * ROWS
    col = lax.broadcasted_iota(I32, (ROWS, TILE), 1)
    inside = [(row < shape[0, b]) & (col < shape[1, b]) for b in range(BLK)]
    prefix[PAIRS] = jnp.zeros((TILE, TILE), BF16)
    for fetch in fetches[:2]:
        fetch.wait()
    diag = diag_rows[...].reshape(BLK, ROWS, TILE)
    given = [psi[h].astype(F32).reshape(2, ROWS, TILE) for h in range(2)]
    start = [jnp.where(inside[b], given[b // 2][b % 2], 0.0) for b in range(BLK)]
    for h in range(2):
        raw_one[h, core, x, y, 0] = jnp.concatenate(start[h * 2 : h * 2 + 2], axis=0).astype(BF16)

    links = Links(send_sem, recv_sem, device_of(x, y, z, 1 - core))
    pl.semaphore_wait(barrier, len(greeted))
    arrived = along_z(links, raw_one.at[:, core, x, y, 0], lambda k: raw_one.at[:, core, x, y, k], at)

    copies = [
        pltpu.make_async_copy(steps_v, steps_s, local_sem.at[8]),
        pltpu.make_async_copy(last_v, last_s, local_sem.at[9]),
    ]

    def plan():
        for fetch in fetches[2:6]:
            fetch.wait()
        schedule(source[0], target[0], left[0], right[0], count[0, 0], steps_v, last_v)
        for copy in copies:
            copy.start()

    start_squares = jnp.sum(gather(links, raw_one, vector, at, arrived, ORDER_ONE, plan), keepdims=True)
    for copy in copies + fetches[6:]:
        copy.wait()
    contract(steps_s, last_s, vector, lefts, rights, prefix, total)

    overlap = jnp.zeros((ROWS, TILE), F32)
    for b in range(BLK):
        overlap = overlap + start[b] * start[b] * diag[b]
        tile = vector[sector * BLK + b].astype(F32).reshape(N_TERM, ROWS, TILE)
        overlap = overlap + jnp.sum(tile * total[b].reshape(N_TERM, ROWS, TILE), axis=0)
    part[0] = overlap
    gathered = list(links.pending)
    sector_sum = everyone(links, part.at[0], part_sector, sector, N_SECTOR, at_sector)
    rows_sum = spread(links, total, out_one, back_one, term, at_term)
    part[1] = sector_sum()
    term_sum = everyone(links, part.at[1], part_term, term, N_TERM, at_term)
    links.drain(gathered)
    coupled = rows_sum()
    sigma = [jnp.where(inside[b], diag[b] * start[b] + coupled[b], 0.0) for b in range(BLK)]
    for b in range(BLK):
        rows_f32[0, b] = sigma[b]
    arrived_f32 = along_z(links, rows_f32.at[0], lambda k: rows_f32.at[k], at)
    for b in range(BLK):
        sigma_one[b] = sigma[b]
    rayleigh = jnp.sum(term_sum(), keepdims=True) / start_squares

    def residual_here(begin, end):
        arrived_f32(begin, end)
        for k in range(begin, end):
            for h in range(2):
                before = raw_one[h, core, x, y, k].astype(F32)
                after = rows_f32[k, h * 2 : h * 2 + 2].reshape(2 * ROWS, TILE)
                raw_two[h, core, x, y, k] = (after - rayleigh * before).astype(BF16)

    squares = jnp.sum(gather(links, raw_two, vector, at, residual_here, ORDER_TWO), keepdims=True)
    scale = lax.rsqrt(squares / float(NBLK * TILE * TILE) + 1e-06)
    contract(steps_s, last_s, vector, lefts, rights, prefix, total)
    gathered = list(links.pending)
    rows_sum = spread(links, total, out_two, back_two, term, at_term)
    links.drain(gathered)
    coupled = rows_sum()
    for b in range(BLK):
        second = raw_two[b // 2, core, x, y, 0].astype(F32)[(b % 2) * ROWS : (b % 2 + 1) * ROWS]
        sigma_two[b] = jnp.where(inside[b], (diag[b] * second + coupled[b]) * scale, 0.0)
    links.drain()


def keep_kernel(one, two, one_out, two_out):
    one_out[...] = one[...]
    two_out[...] = two[...]


def body(psi, diag_energy, block_shape, *rest):
    vmem = pl.BlockSpec(memory_space=pltpu.VMEM)
    smem = pl.BlockSpec(memory_space=pltpu.SMEM)
    hbm = pl.BlockSpec(memory_space=pltpu.HBM)
    out = jax.ShapeDtypeStruct((BLK, ROWS, TILE), F32)
    raw = pltpu.VMEM((2, NCORE, NX, NY, NZ, 2 * ROWS, TILE), BF16)
    rows = pltpu.VMEM((N_TERM, 2, 2 * ROWS, TILE), BF16)
    slots = pltpu.VMEM((1, 1, PAIRS), I32)
    sums = pl.pallas_call(
        kernel,
        out_shape=(out, out),
        in_specs=[hbm, hbm, smem, hbm, hbm, hbm, hbm, hbm, hbm, smem],
        out_specs=(vmem, vmem),
        scratch_shapes=[
            pltpu.VMEM((2, 2 * ROWS, TILE), BF16),
            pltpu.VMEM((BLK * ROWS, TILE), F32),
            slots,
            slots,
            slots,
            slots,
            raw,
            raw,
            pltpu.VMEM((NZ, BLK, ROWS, TILE), F32),
            pltpu.VMEM((NBLK, NZ, 2 * ROWS, TILE), BF16),
            pltpu.VMEM((ENV, TILE, TILE), BF16),
            pltpu.VMEM((ENV, TILE, TILE), BF16),
            pltpu.VMEM((PAIRS + 1, TILE, TILE), BF16),
            pltpu.VMEM((BLK, TILE, TILE), F32),
            rows,
            rows,
            rows,
            rows,
            pltpu.VMEM((2, ROWS, TILE), F32),
            pltpu.VMEM((N_SECTOR, ROWS, TILE), F32),
            pltpu.VMEM((N_TERM, ROWS, TILE), F32),
            pltpu.VMEM((8, PAIRS), I32),
            pltpu.VMEM((8, TILE), I32),
            pltpu.SMEM((8, PAIRS), I32),
            pltpu.SMEM((8, TILE), I32),
            pltpu.SemaphoreType.DMA((10,)),
            pltpu.SemaphoreType.DMA((N_SEND,)),
            pltpu.SemaphoreType.DMA((N_SEND,)),
        ],
        compiler_params=pltpu.CompilerParams(
            collective_id=0, has_side_effects=True, vmem_limit_bytes=60 * 2**20
        ),
        name="two_products",
    )(psi.reshape(2, 2 * ROWS, TILE), diag_energy.reshape(BLK * ROWS, TILE), block_shape.T, *rest)
    return pl.pallas_call(
        keep_kernel,
        out_shape=(out, out),
        in_specs=[vmem, vmem],
        out_specs=(vmem, vmem),
        name="keep",
    )(*sums)


def solution(mesh):
    placed = (
        P("sector", "term", None),
        P("sector", "term", None),
        P("sector", None),
        P("term", "sector", None, None, None),
        P("term", "sector", None, None, None),
        P("term", "sector", None),
        P("term", "sector", None),
        P("term", "sector", None),
        P("term", "sector", None),
        P("term", "sector"),
    )
    return jax.shard_map(
        body,
        mesh=mesh,
        in_specs=placed,
        out_specs=(P("sector", "term", None), P("sector", "term", None)),
        check_vma=False,
    )
```

```python
import functools

import jax
import jax.numpy as jnp
from jax import lax
from jax.experimental import pallas as pl
from jax.experimental.pallas import tpu as pltpu
from jax.sharding import PartitionSpec as P

F32 = jnp.float32
BF16 = jnp.bfloat16
I32 = jnp.int32
MESH = pl.DeviceIdType.MESH

TILE = 128
PAIRS = 384
ENV = 32
BLK = 4
ROWS = 8
NX, NY, NZ, NCORE = 4, 4, 8, 2
N_TERM, N_SECTOR = 16, 16
NBLK = N_SECTOR * BLK
GROUPS = ENV * BLK
UNROLL = 384
N_SEND = 64
OFFSETS = (0, 1, -1, 2, -2, 3, -3, 4)
ZGROUPS = ((0, 1), (1, 3), (3, 5), (5, 7), (7, 8))


def order_of(*marks):
    names = {"n": "near", "f": "far", "h": "hand", "t": "take", "a": "aside"}
    return tuple((names[mark[0]], int(mark[1:])) for mark in marks)


ENDS = ("h0", "h1", "t0", "h2", "t1", "h3", "t2", "h4", "t3", "t4")
ORDER_ONE = order_of("n0", "a0", "n1", "n2", "f0", "n3", "n4", "f1", "f2", "f3", "f4", *ENDS)
ORDER_TWO = order_of("n0", "n1", "n2", "n3", "n4", "f0", "f1", "f2", "f3", "f4", *ENDS)
NT = (((1,), (1,)), ((), ()))


def dot(a, b):
    return jnp.dot(a, b, preferred_element_type=F32)


def as_bf16(flags):
    return flags.astype(F32).astype(BF16)


def schedule(source, target, left, right, count, steps_ref, last_ref):
    slot = lax.broadcasted_iota(I32, (1, PAIRS), 1)
    live = slot < count
    key = jnp.where(live, left * BLK + target, GROUPS)
    member = lax.broadcasted_iota(I32, (GROUPS, PAIRS), 0) == key
    member_f = member.astype(F32)
    member_b = member_f.astype(BF16)
    earlier = as_bf16(
        lax.broadcasted_iota(I32, (PAIRS, PAIRS), 0) < lax.broadcasted_iota(I32, (PAIRS, PAIRS), 1)
    )
    rank = jnp.sum(member_f * dot(member_b, earlier), axis=0, keepdims=True)
    row_g = lax.broadcasted_iota(I32, (GROUPS, GROUPS), 0)
    col_g = lax.broadcasted_iota(I32, (GROUPS, GROUPS), 1)
    size = jnp.broadcast_to(jnp.sum(member_f, axis=1, keepdims=True), (GROUPS, GROUPS))
    high = jnp.floor(size * (1.0 / 16.0))
    low = size - 16.0 * high
    below = as_bf16(col_g < row_g)
    begin = 16.0 * dot(below, high.astype(BF16)) + dot(below, low.astype(BF16))
    begin_of = jnp.sum(member_f * begin[:, :1], axis=0, keepdims=True)
    place = jnp.where(live, (rank + begin_of).astype(I32), -1)
    sent = as_bf16(lax.broadcasted_iota(I32, (PAIRS, PAIRS), 0) == place)
    line = lax.broadcasted_iota(I32, (8, PAIRS), 0)
    table = jnp.where(line == 0, source, jnp.where(line == 1, right, jnp.where(line == 2, key, 0)))
    moved = lax.dot_general(table.astype(F32).astype(BF16), sent, NT, preferred_element_type=F32)
    again = (moved == pltpu.roll(moved, 1, 1)) & (lax.broadcasted_iota(I32, (8, PAIRS), 1) > 0)
    top = jnp.where(line == 0, NBLK - 1, jnp.where(line == 1, ENV - 1, 1))
    steps_ref[...] = jnp.clip(jnp.where(line == 2, again.astype(I32), moved.astype(I32)), 0, top)
    size = lax.dot_general(jnp.ones((8, PAIRS), BF16), member_b, NT, preferred_element_type=F32)
    high = jnp.floor(size * (1.0 / 16.0))
    low = size - 16.0 * high
    above = as_bf16(row_g < col_g)
    begin = 16.0 * dot(high.astype(BF16), above) + dot(low.astype(BF16), above)
    ends = (begin + size).astype(I32) - 1
    last_ref[...] = jnp.where(size > 0.5, jnp.clip(ends, 0, PAIRS - 1), PAIRS)


def contract(steps, last, vector, lefts, rights, prefix, total):
    def step_body(turn, running):
        for u in range(UNROLL):
            k = turn * UNROLL + u
            keep = steps[2, k].astype(F32)
            tile = vector[steps[0, k]].reshape(TILE, TILE)
            running = running * keep + dot(tile, rights[steps[1, k]])
            prefix[k] = running.astype(BF16)
        return running

    lax.fori_loop(0, PAIRS // UNROLL, step_body, jnp.zeros((TILE, TILE), F32))
    for half in range(2):
        running = jnp.zeros((TILE, 2 * TILE), F32)
        for l in range(0, ENV, 2):
            tiles = jnp.concatenate([lefts[l], lefts[l + 1]], axis=1)
            sums = [
                jnp.concatenate([prefix[last[0, (l + dl) * BLK + half * 2 + db]] for db in range(2)], axis=1)
                for dl in range(2)
            ]
            running = running + dot(tiles, jnp.concatenate(sums, axis=0))
        total[half * 2] = running[:, :TILE]
        total[half * 2 + 1] = running[:, TILE:]


def device_of(x, y, z, core):
    return (z * 2 + lax.div(y, 2), x * 4 + lax.rem(y, 2) * 2 + core)


class Links:
    def __init__(self, send_sem, recv_sem, device):
        self.send_sem, self.recv_sem, self.device = send_sem, recv_sem, device
        self.used = 0
        self.pending = []

    def slot(self, whole):
        self.used += 1
        self.pending.append((whole, self.used - 1))
        return self.used - 1

    def copy(self, ref, slot, device, dst=None):
        return pltpu.make_async_remote_copy(
            src_ref=ref,
            dst_ref=ref if dst is None else dst,
            send_sem=self.send_sem.at[slot],
            recv_sem=self.recv_sem.at[slot],
            device_id=device,
            device_id_type=MESH,
        )

    def send(self, ref, slot, device, dst=None):
        self.copy(ref, slot, device, dst).start()

    def arrived(self, whole, slot):
        self.copy(whole, slot, self.device).wait_recv()

    def drain(self, pending=None):
        for whole, slot in list(self.pending) if pending is None else pending:
            self.copy(whole, slot, self.device).wait_send()
            self.pending.remove((whole, slot))


def gather(links, raw, vector, at, ready, order, aside=None):
    x, y, z, core = at
    mate = device_of(x, y, z, 1 - core)
    squares = jnp.zeros((ROWS, TILE), F32)

    def wrap(i):
        return lax.rem(i, 4)

    def along_x(step):
        return device_of(wrap(x + step), y, z, core)

    def along_y(step):
        return device_of(x, wrap(y + step), z, core)

    def exchange(along, mine, three):
        slot = links.slot(three)
        for d in (2, 1, 3):
            links.send(mine, slot, along(d))
        return lambda: links.arrived(three, slot)

    others = pl.ds(0, 3)
    state = [None] * len(ZGROUPS)
    for event, i in order:
        begin, end = ZGROUPS[i]
        g = pl.ds(begin, end - begin)
        if event == "aside":
            aside()
        elif event == "near":
            ready(begin, end)
            state[i] = (
                exchange(along_y, raw.at[0, core, x, y, g], raw.at[0, core, x, others, g]),
                exchange(along_x, raw.at[1, core, x, y, g], raw.at[1, core, others, y, g]),
            )
        elif event == "far":
            wait_y, wait_x = state[i]
            wait_y()
            first = exchange(along_x, raw.at[0, core, x, :, g], raw.at[0, core, others, :, g])
            wait_x()
            second = exchange(along_y, raw.at[1, core, :, y, g], raw.at[1, core, :, others, g])
            state[i] = (first, second)
        elif event == "hand":
            for wait in state[i]:
                wait()
            here = raw.at[:, core, :, :, g]
            state[i] = links.slot(here)
            links.send(here, state[i], mate)
            squares = settle(raw, vector, z, core, begin, end, squares)
        else:
            links.arrived(raw.at[:, 1 - core, :, :, g], state[i])
            squares = settle(raw, vector, z, 1 - core, begin, end, squares)
    return squares


def settle(raw, vector, z, core, begin, end, squares):
    def body(x, squares):
        for h in range(2):
            for y_lo in range(2):
                block = (x * 4 + y_lo * 2 + core) * BLK + h * 2
                for k in range(begin, end):
                    origin = lax.rem(z + (OFFSETS[k] + NZ), NZ)
                    low = raw[h, core, x, y_lo, k].astype(F32)
                    high = raw[h, core, x, y_lo + 2, k].astype(F32)
                    squares = squares + (low[:ROWS] * low[:ROWS] + low[ROWS:] * low[ROWS:])
                    squares = squares + (high[:ROWS] * high[:ROWS] + high[ROWS:] * high[ROWS:])
                    vector[block, origin] = jnp.concatenate([low[:ROWS], high[:ROWS]], axis=0).astype(BF16)
                    vector[block + 1, origin] = jnp.concatenate([low[ROWS:], high[ROWS:]], axis=0).astype(BF16)
        return squares

    return lax.fori_loop(0, NX, body, squares)


def along_z(links, mine, place, at):
    x, y, z, core = at
    slots = [links.slot(place(pl.ds(max(begin, 1), end - max(begin, 1)))) if end > 1 else None for begin, end in ZGROUPS]
    group = [i for i, (begin, end) in enumerate(ZGROUPS) for _ in range(begin, end)]
    for k in range(1, NZ):
        to = device_of(x, y, lax.rem(z - OFFSETS[k] + NZ, NZ), core)
        links.send(mine, slots[group[k]], to, place(k))

    def wait(begin, end):
        slot = slots[group[begin]]
        if slot is not None:
            begin = max(begin, 1)
            links.arrived(place(pl.ds(begin, end - begin)), slot)

    return wait


def spread(links, total, out, back, me, at_term):
    for h in range(2):
        rows = [total[h * 2 + k].reshape(N_TERM, ROWS, TILE) for k in range(2)]
        both = jnp.stack(rows, axis=1).reshape(N_TERM, 2 * ROWS, TILE).astype(BF16)
        out[:, h] = both
    peers = pl.ds(1, N_TERM - 1)
    slot = links.slot(back.at[peers])
    for d in sorted(range(1, N_TERM), key=lambda d: abs(d - N_TERM // 2)):
        peer = lax.rem(me + d, N_TERM)
        links.send(out.at[peer], slot, at_term(peer), back.at[d])

    def wait():
        acc = out[me].astype(F32)
        links.arrived(back.at[peers], slot)
        return (acc + jnp.sum(back[peers].astype(F32), axis=0)).reshape(BLK, ROWS, TILE)

    return wait


def everyone(links, mine, back, here, n, at):
    peers = pl.ds(1, n - 1)
    slot = links.slot(back.at[peers])
    for d in sorted(range(1, n), key=lambda d: abs(d - n // 2)):
        links.send(mine, slot, at(lax.rem(here + d, n)), back.at[d])

    def wait():
        acc = mine[...]
        links.arrived(back.at[peers], slot)
        return acc + jnp.sum(back[peers], axis=0)

    return wait


def kernel(
    psi_hbm,
    diag_hbm,
    shape,
    env_left,
    env_right,
    source_hbm,
    target_hbm,
    left_hbm,
    right_hbm,
    count,
    sigma_one,
    sigma_two,
    psi,
    diag_rows,
    source,
    target,
    left,
    right,
    raw_one,
    raw_two,
    rows_f32,
    vector,
    lefts,
    rights,
    prefix,
    total,
    out_one,
    out_two,
    back_one,
    back_two,
    part,
    part_sector,
    part_term,
    steps_v,
    last_v,
    steps_s,
    last_s,
    local_sem,
    send_sem,
    recv_sem,
):
    term, sector = lax.axis_index("term"), lax.axis_index("sector")
    z, y_hi = lax.div(term, 2), lax.rem(term, 2)
    x, y_lo, core = lax.div(sector, 4), lax.rem(lax.div(sector, 2), 2), lax.rem(sector, 2)
    y = y_hi * 2 + y_lo
    at = (x, y, z, core)

    def at_term(t):
        return (t, sector)

    def at_sector(s):
        return (term, s)

    fetches = [
        pltpu.make_async_copy(here, there, local_sem.at[i])
        for i, (here, there) in enumerate(
            (
                (psi_hbm, psi),
                (diag_hbm, diag_rows),
                (source_hbm, source),
                (target_hbm, target),
                (left_hbm, left),
                (right_hbm, right),
                (env_left.at[0, 0], lefts),
                (env_right.at[0, 0], rights),
            )
        )
    ]
    for fetch in fetches[:2]:
        fetch.start()

    barrier = pltpu.get_barrier_semaphore()
    greeted = [at_term(lax.rem(term + d, N_TERM)) for d in range(1, N_TERM)]
    greeted += [at_sector(lax.rem(sector + d, N_SECTOR)) for d in range(1, N_SECTOR)]
    chip = lax.div(sector, 2)
    greeted += [(z * 2 + 1 - y_hi, lax.rem(chip + d, N_SECTOR // 2) * 2 + core) for d in range(1, N_SECTOR // 2)]
    for device in greeted:
        pl.semaphore_signal(barrier, inc=1, device_id=device, device_id_type=MESH)
    for fetch in fetches[2:]:
        fetch.start()

    row = lax.broadcasted_iota(I32, (ROWS, TILE), 0) + term * ROWS
    col = lax.broadcasted_iota(I32, (ROWS, TILE), 1)
    inside = [(row < shape[0, b]) & (col < shape[1, b]) for b in range(BLK)]
    prefix[PAIRS] = jnp.zeros((TILE, TILE), BF16)
    for fetch in fetches[:2]:
        fetch.wait()
    diag = diag_rows[...].reshape(BLK, ROWS, TILE)
    given = [psi[h].astype(F32).reshape(2, ROWS, TILE) for h in range(2)]
    start = [jnp.where(inside[b], given[b // 2][b % 2], 0.0) for b in range(BLK)]
    for h in range(2):
        raw_one[h, core, x, y, 0] = jnp.concatenate(start[h * 2 : h * 2 + 2], axis=0).astype(BF16)

    links = Links(send_sem, recv_sem, device_of(x, y, z, 1 - core))
    pl.semaphore_wait(barrier, len(greeted))
    arrived = along_z(links, raw_one.at[:, core, x, y, 0], lambda k: raw_one.at[:, core, x, y, k], at)

    copies = [
        pltpu.make_async_copy(steps_v, steps_s, local_sem.at[8]),
        pltpu.make_async_copy(last_v, last_s, local_sem.at[9]),
    ]

    def plan():
        for fetch in fetches[2:6]:
            fetch.wait()
        schedule(source[0], target[0], left[0], right[0], count[0, 0], steps_v, last_v)
        for copy in copies:
            copy.start()

    start_squares = jnp.sum(gather(links, raw_one, vector, at, arrived, ORDER_ONE, plan), keepdims=True)
    for copy in copies + fetches[6:]:
        copy.wait()
    contract(steps_s, last_s, vector, lefts, rights, prefix, total)

    overlap = jnp.zeros((ROWS, TILE), F32)
    for b in range(BLK):
        overlap = overlap + start[b] * start[b] * diag[b]
        tile = vector[sector * BLK + b].astype(F32).reshape(N_TERM, ROWS, TILE)
        overlap = overlap + jnp.sum(tile * total[b].reshape(N_TERM, ROWS, TILE), axis=0)
    part[0] = overlap
    gathered = list(links.pending)
    sector_sum = everyone(links, part.at[0], part_sector, sector, N_SECTOR, at_sector)
    rows_sum = spread(links, total, out_one, back_one, term, at_term)
    part[1] = sector_sum()
    term_sum = everyone(links, part.at[1], part_term, term, N_TERM, at_term)
    links.drain(gathered)
    coupled = rows_sum()
    sigma = [jnp.where(inside[b], diag[b] * start[b] + coupled[b], 0.0) for b in range(BLK)]
    for b in range(BLK):
        rows_f32[0, b] = sigma[b]
    arrived_f32 = along_z(links, rows_f32.at[0], lambda k: rows_f32.at[k], at)
    for b in range(BLK):
        sigma_one[b] = sigma[b]
    rayleigh = jnp.sum(term_sum(), keepdims=True) / start_squares

    def residual_here(begin, end):
        arrived_f32(begin, end)
        for k in range(begin, end):
            for h in range(2):
                before = raw_one[h, core, x, y, k].astype(F32)
                after = rows_f32[k, h * 2 : h * 2 + 2].reshape(2 * ROWS, TILE)
                raw_two[h, core, x, y, k] = (after - rayleigh * before).astype(BF16)

    squares = jnp.sum(gather(links, raw_two, vector, at, residual_here, ORDER_TWO), keepdims=True)
    scale = lax.rsqrt(squares / float(NBLK * TILE * TILE) + 1e-06)
    contract(steps_s, last_s, vector, lefts, rights, prefix, total)
    gathered = list(links.pending)
    rows_sum = spread(links, total, out_two, back_two, term, at_term)
    links.drain(gathered)
    coupled = rows_sum()
    for b in range(BLK):
        second = raw_two[b // 2, core, x, y, 0].astype(F32)[(b % 2) * ROWS : (b % 2 + 1) * ROWS]
        sigma_two[b] = jnp.where(inside[b], (diag[b] * second + coupled[b]) * scale, 0.0)
    links.drain()


def keep_kernel(one, two, one_out, two_out):
    one_out[...] = one[...]
    two_out[...] = two[...]


def body(psi, diag_energy, block_shape, *rest):
    vmem = pl.BlockSpec(memory_space=pltpu.VMEM)
    smem = pl.BlockSpec(memory_space=pltpu.SMEM)
    hbm = pl.BlockSpec(memory_space=pltpu.HBM)
    out = jax.ShapeDtypeStruct((BLK, ROWS, TILE), F32)
    raw = pltpu.VMEM((2, NCORE, NX, NY, NZ, 2 * ROWS, TILE), BF16)
    rows = pltpu.VMEM((N_TERM, 2, 2 * ROWS, TILE), BF16)
    slots = pltpu.VMEM((1, 1, PAIRS), I32)
    sums = pl.pallas_call(
        kernel,
        out_shape=(out, out),
        in_specs=[hbm, hbm, smem, hbm, hbm, hbm, hbm, hbm, hbm, smem],
        out_specs=(vmem, vmem),
        scratch_shapes=[
            pltpu.VMEM((2, 2 * ROWS, TILE), BF16),
            pltpu.VMEM((BLK * ROWS, TILE), F32),
            slots,
            slots,
            slots,
            slots,
            raw,
            raw,
            pltpu.VMEM((NZ, BLK, ROWS, TILE), F32),
            pltpu.VMEM((NBLK, NZ, 2 * ROWS, TILE), BF16),
            pltpu.VMEM((ENV, TILE, TILE), BF16),
            pltpu.VMEM((ENV, TILE, TILE), BF16),
            pltpu.VMEM((PAIRS + 1, TILE, TILE), BF16),
            pltpu.VMEM((BLK, TILE, TILE), F32),
            rows,
            rows,
            rows,
            rows,
            pltpu.VMEM((2, ROWS, TILE), F32),
            pltpu.VMEM((N_SECTOR, ROWS, TILE), F32),
            pltpu.VMEM((N_TERM, ROWS, TILE), F32),
            pltpu.VMEM((8, PAIRS), I32),
            pltpu.VMEM((8, TILE), I32),
            pltpu.SMEM((8, PAIRS), I32),
            pltpu.SMEM((8, TILE), I32),
            pltpu.SemaphoreType.DMA((10,)),
            pltpu.SemaphoreType.DMA((N_SEND,)),
            pltpu.SemaphoreType.DMA((N_SEND,)),
        ],
        compiler_params=pltpu.CompilerParams(
            collective_id=0, has_side_effects=True, vmem_limit_bytes=60 * 2**20
        ),
        name="two_products",
    )(psi.reshape(2, 2 * ROWS, TILE), diag_energy.reshape(BLK * ROWS, TILE), block_shape.T, *rest)
    return pl.pallas_call(
        keep_kernel,
        out_shape=(out, out),
        in_specs=[vmem, vmem],
        out_specs=(vmem, vmem),
        name="keep",
    )(*sums)


def solution(mesh):
    placed = (
        P("sector", "term", None),
        P("sector", "term", None),
        P("sector", None),
        P("term", "sector", None, None, None),
        P("term", "sector", None, None, None),
        P("term", "sector", None),
        P("term", "sector", None),
        P("term", "sector", None),
        P("term", "sector", None),
        P("term", "sector"),
    )
    return jax.shard_map(
        body,
        mesh=mesh,
        in_specs=placed,
        out_specs=(P("sector", "term", None), P("sector", "term", None)),
        check_vma=False,
    )
```

```python
import functools

import jax
import jax.numpy as jnp
from jax import lax
from jax.experimental import pallas as pl
from jax.experimental.pallas import tpu as pltpu
from jax.sharding import PartitionSpec as P

F32 = jnp.float32
BF16 = jnp.bfloat16
I32 = jnp.int32
MESH = pl.DeviceIdType.MESH

TILE = 128
PAIRS = 384
ENV = 32
BLK = 4
ROWS = 8
NX, NY, NZ, NCORE = 4, 4, 8, 2
N_TERM, N_SECTOR = 16, 16
NBLK = N_SECTOR * BLK
GROUPS = ENV * BLK
UNROLL = 384
N_SEND = 64
OFFSETS = (0, 1, -1, 2, -2, 3, -3, 4)
ZGROUPS = ((0, 1), (1, 3), (3, 5), (5, 7), (7, 8))


def order_of(*marks):
    names = {"n": "near", "f": "far", "h": "hand", "t": "take", "a": "aside"}
    return tuple((names[mark[0]], int(mark[1:])) for mark in marks)


ENDS = ("h0", "h1", "t0", "h2", "t1", "h3", "t2", "h4", "t3", "t4")
ORDER_ONE = order_of("n0", "a0", "n1", "n2", "f0", "n3", "n4", "f1", "f2", "f3", "f4", *ENDS)
ORDER_TWO = order_of("n0", "n1", "n2", "n3", "n4", "f0", "f1", "f2", "f3", "f4", *ENDS)
NT = (((1,), (1,)), ((), ()))


def dot(a, b):
    return jnp.dot(a, b, preferred_element_type=F32)


def as_bf16(flags):
    return flags.astype(F32).astype(BF16)


def schedule(source, target, left, right, count, steps_ref, last_ref):
    slot = lax.broadcasted_iota(I32, (1, PAIRS), 1)
    live = slot < count
    key = jnp.where(live, left * BLK + target, GROUPS)
    member = lax.broadcasted_iota(I32, (GROUPS, PAIRS), 0) == key
    member_f = member.astype(F32)
    member_b = member_f.astype(BF16)
    earlier = as_bf16(
        lax.broadcasted_iota(I32, (PAIRS, PAIRS), 0) < lax.broadcasted_iota(I32, (PAIRS, PAIRS), 1)
    )
    rank = jnp.sum(member_f * dot(member_b, earlier), axis=0, keepdims=True)
    row_g = lax.broadcasted_iota(I32, (GROUPS, GROUPS), 0)
    col_g = lax.broadcasted_iota(I32, (GROUPS, GROUPS), 1)
    size = jnp.broadcast_to(jnp.sum(member_f, axis=1, keepdims=True), (GROUPS, GROUPS))
    high = jnp.floor(size * (1.0 / 16.0))
    low = size - 16.0 * high
    below = as_bf16(col_g < row_g)
    begin = 16.0 * dot(below, high.astype(BF16)) + dot(below, low.astype(BF16))
    begin_of = jnp.sum(member_f * begin[:, :1], axis=0, keepdims=True)
    place = jnp.where(live, (rank + begin_of).astype(I32), -1)
    sent = as_bf16(lax.broadcasted_iota(I32, (PAIRS, PAIRS), 0) == place)
    line = lax.broadcasted_iota(I32, (8, PAIRS), 0)
    table = jnp.where(line == 0, source, jnp.where(line == 1, right, jnp.where(line == 2, key, 0)))
    moved = lax.dot_general(table.astype(F32).astype(BF16), sent, NT, preferred_element_type=F32)
    again = (moved == pltpu.roll(moved, 1, 1)) & (lax.broadcasted_iota(I32, (8, PAIRS), 1) > 0)
    top = jnp.where(line == 0, NBLK - 1, jnp.where(line == 1, ENV - 1, 1))
    steps_ref[...] = jnp.clip(jnp.where(line == 2, again.astype(I32), moved.astype(I32)), 0, top)
    size = lax.dot_general(jnp.ones((8, PAIRS), BF16), member_b, NT, preferred_element_type=F32)
    high = jnp.floor(size * (1.0 / 16.0))
    low = size - 16.0 * high
    above = as_bf16(row_g < col_g)
    begin = 16.0 * dot(high.astype(BF16), above) + dot(low.astype(BF16), above)
    ends = (begin + size).astype(I32) - 1
    last_ref[...] = jnp.where(size > 0.5, jnp.clip(ends, 0, PAIRS - 1), PAIRS)


def contract(steps, last, vector, lefts, rights, prefix, total):
    def step_body(turn, running):
        for u in range(UNROLL):
            k = turn * UNROLL + u
            keep = steps[2, k].astype(F32)
            tile = vector[steps[0, k]].reshape(TILE, TILE)
            running = running * keep + dot(tile, rights[steps[1, k]])
            prefix[k] = running.astype(BF16)
        return running

    lax.fori_loop(0, PAIRS // UNROLL, step_body, jnp.zeros((TILE, TILE), F32))
    for half in range(2):
        running = jnp.zeros((TILE, 2 * TILE), F32)
        for l in range(0, ENV, 2):
            tiles = jnp.concatenate([lefts[l], lefts[l + 1]], axis=1)
            sums = [
                jnp.concatenate([prefix[last[0, (l + dl) * BLK + half * 2 + db]] for db in range(2)], axis=1)
                for dl in range(2)
            ]
            running = running + dot(tiles, jnp.concatenate(sums, axis=0))
        total[half * 2] = running[:, :TILE]
        total[half * 2 + 1] = running[:, TILE:]


def device_of(x, y, z, core):
    return (z * 2 + lax.div(y, 2), x * 4 + lax.rem(y, 2) * 2 + core)


class Links:
    def __init__(self, send_sem, recv_sem, device):
        self.send_sem, self.recv_sem, self.device = send_sem, recv_sem, device
        self.used = 0
        self.pending = []

    def slot(self, whole):
        self.used += 1
        self.pending.append((whole, self.used - 1))
        return self.used - 1

    def copy(self, ref, slot, device, dst=None):
        return pltpu.make_async_remote_copy(
            src_ref=ref,
            dst_ref=ref if dst is None else dst,
            send_sem=self.send_sem.at[slot],
            recv_sem=self.recv_sem.at[slot],
            device_id=device,
            device_id_type=MESH,
        )

    def send(self, ref, slot, device, dst=None):
        self.copy(ref, slot, device, dst).start()

    def arrived(self, whole, slot):
        self.copy(whole, slot, self.device).wait_recv()

    def drain(self, pending=None):
        for whole, slot in list(self.pending) if pending is None else pending:
            self.copy(whole, slot, self.device).wait_send()
            self.pending.remove((whole, slot))


def gather(links, raw, vector, at, ready, order, aside=None):
    x, y, z, core = at
    mate = device_of(x, y, z, 1 - core)
    squares = jnp.zeros((ROWS, TILE), F32)

    def wrap(i):
        return lax.rem(i, 4)

    def along_x(step):
        return device_of(wrap(x + step), y, z, core)

    def along_y(step):
        return device_of(x, wrap(y + step), z, core)

    def exchange(along, mine, three):
        slot = links.slot(three)
        for d in (2, 1, 3):
            links.send(mine, slot, along(d))
        return lambda: links.arrived(three, slot)

    others = pl.ds(0, 3)
    state = [None] * len(ZGROUPS)
    for event, i in order:
        begin, end = ZGROUPS[i]
        g = pl.ds(begin, end - begin)
        if event == "aside":
            aside()
        elif event == "near":
            ready(begin, end)
            state[i] = (
                exchange(along_y, raw.at[0, core, x, y, g], raw.at[0, core, x, others, g]),
                exchange(along_x, raw.at[1, core, x, y, g], raw.at[1, core, others, y, g]),
            )
        elif event == "far":
            wait_y, wait_x = state[i]
            wait_y()
            first = exchange(along_x, raw.at[0, core, x, :, g], raw.at[0, core, others, :, g])
            wait_x()
            second = exchange(along_y, raw.at[1, core, :, y, g], raw.at[1, core, :, others, g])
            state[i] = (first, second)
        elif event == "hand":
            for wait in state[i]:
                wait()
            here = raw.at[:, core, :, :, g]
            state[i] = links.slot(here)
            links.send(here, state[i], mate)
            squares = settle(raw, vector, z, core, begin, end, squares)
        else:
            links.arrived(raw.at[:, 1 - core, :, :, g], state[i])
            squares = settle(raw, vector, z, 1 - core, begin, end, squares)
    return squares


def settle(raw, vector, z, core, begin, end, squares):
    def body(x, squares):
        for h in range(2):
            for y_lo in range(2):
                block = (x * 4 + y_lo * 2 + core) * BLK + h * 2
                for k in range(begin, end):
                    origin = lax.rem(z + (OFFSETS[k] + NZ), NZ)
                    low = raw[h, core, x, y_lo, k].astype(F32)
                    high = raw[h, core, x, y_lo + 2, k].astype(F32)
                    squares = squares + (low[:ROWS] * low[:ROWS] + low[ROWS:] * low[ROWS:])
                    squares = squares + (high[:ROWS] * high[:ROWS] + high[ROWS:] * high[ROWS:])
                    vector[block, origin] = jnp.concatenate([low[:ROWS], high[:ROWS]], axis=0).astype(BF16)
                    vector[block + 1, origin] = jnp.concatenate([low[ROWS:], high[ROWS:]], axis=0).astype(BF16)
        return squares

    return lax.fori_loop(0, NX, body, squares)


def along_z(links, mine, place, at):
    x, y, z, core = at
    slots = [links.slot(place(pl.ds(max(begin, 1), end - max(begin, 1)))) if end > 1 else None for begin, end in ZGROUPS]
    group = [i for i, (begin, end) in enumerate(ZGROUPS) for _ in range(begin, end)]
    for k in range(1, NZ):
        to = device_of(x, y, lax.rem(z - OFFSETS[k] + NZ, NZ), core)
        links.send(mine, slots[group[k]], to, place(k))

    def wait(begin, end):
        slot = slots[group[begin]]
        if slot is not None:
            begin = max(begin, 1)
            links.arrived(place(pl.ds(begin, end - begin)), slot)

    return wait


def spread(links, total, out, back, me, at_term):
    for h in range(2):
        rows = [total[h * 2 + k].reshape(N_TERM, ROWS, TILE) for k in range(2)]
        both = jnp.stack(rows, axis=1).reshape(N_TERM, 2 * ROWS, TILE).astype(BF16)
        out[:, h] = both
    peers = pl.ds(1, N_TERM - 1)
    slot = links.slot(back.at[peers])
    for d in sorted(range(1, N_TERM), key=lambda d: abs(d - N_TERM // 2)):
        peer = lax.rem(me + d, N_TERM)
        links.send(out.at[peer], slot, at_term(peer), back.at[d])

    def wait():
        acc = out[me].astype(F32)
        links.arrived(back.at[peers], slot)
        return (acc + jnp.sum(back[peers].astype(F32), axis=0)).reshape(BLK, ROWS, TILE)

    return wait


def everyone(links, mine, back, here, n, at):
    peers = pl.ds(1, n - 1)
    slot = links.slot(back.at[peers])
    for d in sorted(range(1, n), key=lambda d: abs(d - n // 2)):
        links.send(mine, slot, at(lax.rem(here + d, n)), back.at[d])

    def wait():
        acc = mine[...]
        links.arrived(back.at[peers], slot)
        return acc + jnp.sum(back[peers], axis=0)

    return wait


def kernel(
    psi_hbm,
    diag_hbm,
    shape,
    env_left,
    env_right,
    source_hbm,
    target_hbm,
    left_hbm,
    right_hbm,
    count,
    sigma_one,
    sigma_two,
    psi,
    diag_rows,
    source,
    target,
    left,
    right,
    raw_one,
    raw_two,
    rows_f32,
    vector,
    lefts,
    rights,
    prefix,
    total,
    out_one,
    out_two,
    back_one,
    back_two,
    part,
    part_sector,
    part_term,
    steps_v,
    last_v,
    steps_s,
    last_s,
    local_sem,
    send_sem,
    recv_sem,
):
    term, sector = lax.axis_index("term"), lax.axis_index("sector")
    z, y_hi = lax.div(term, 2), lax.rem(term, 2)
    x, y_lo, core = lax.div(sector, 4), lax.rem(lax.div(sector, 2), 2), lax.rem(sector, 2)
    y = y_hi * 2 + y_lo
    at = (x, y, z, core)

    def at_term(t):
        return (t, sector)

    def at_sector(s):
        return (term, s)

    fetches = [
        pltpu.make_async_copy(here, there, local_sem.at[i])
        for i, (here, there) in enumerate(
            (
                (psi_hbm, psi),
                (diag_hbm, diag_rows),
                (source_hbm, source),
                (target_hbm, target),
                (left_hbm, left),
                (right_hbm, right),
                (env_left.at[0, 0], lefts),
                (env_right.at[0, 0], rights),
            )
        )
    ]
    for fetch in fetches[:2]:
        fetch.start()

    barrier = pltpu.get_barrier_semaphore()
    greeted = [at_term(lax.rem(term + d, N_TERM)) for d in range(1, N_TERM)]
    greeted += [at_sector(lax.rem(sector + d, N_SECTOR)) for d in range(1, N_SECTOR)]
    chip = lax.div(sector, 2)
    greeted += [(z * 2 + 1 - y_hi, lax.rem(chip + d, N_SECTOR // 2) * 2 + core) for d in range(1, N_SECTOR // 2)]
    for device in greeted:
        pl.semaphore_signal(barrier, inc=1, device_id=device, device_id_type=MESH)
    for fetch in fetches[2:]:
        fetch.start()

    row = lax.broadcasted_iota(I32, (ROWS, TILE), 0) + term * ROWS
    col = lax.broadcasted_iota(I32, (ROWS, TILE), 1)
    inside = [(row < shape[0, b]) & (col < shape[1, b]) for b in range(BLK)]
    prefix[PAIRS] = jnp.zeros((TILE, TILE), BF16)
    for fetch in fetches[:2]:
        fetch.wait()
    diag = diag_rows[...].reshape(BLK, ROWS, TILE)
    given = [psi[h].astype(F32).reshape(2, ROWS, TILE) for h in range(2)]
    start = [jnp.where(inside[b], given[b // 2][b % 2], 0.0) for b in range(BLK)]
    for h in range(2):
        raw_one[h, core, x, y, 0] = jnp.concatenate(start[h * 2 : h * 2 + 2], axis=0).astype(BF16)

    links = Links(send_sem, recv_sem, device_of(x, y, z, 1 - core))
    pl.semaphore_wait(barrier, len(greeted))
    arrived = along_z(links, raw_one.at[:, core, x, y, 0], lambda k: raw_one.at[:, core, x, y, k], at)

    copies = [
        pltpu.make_async_copy(steps_v, steps_s, local_sem.at[8]),
        pltpu.make_async_copy(last_v, last_s, local_sem.at[9]),
    ]

    def plan():
        for fetch in fetches[2:6]:
            fetch.wait()
        schedule(source[0], target[0], left[0], right[0], count[0, 0], steps_v, last_v)
        for copy in copies:
            copy.start()

    start_squares = jnp.sum(gather(links, raw_one, vector, at, arrived, ORDER_ONE, plan), keepdims=True)
    for copy in copies + fetches[6:]:
        copy.wait()
    contract(steps_s, last_s, vector, lefts, rights, prefix, total)

    overlap = jnp.zeros((ROWS, TILE), F32)
    for b in range(BLK):
        overlap = overlap + start[b] * start[b] * diag[b]
        tile = vector[sector * BLK + b].astype(F32).reshape(N_TERM, ROWS, TILE)
        overlap = overlap + jnp.sum(tile * total[b].reshape(N_TERM, ROWS, TILE), axis=0)
    part[0] = overlap
    gathered = list(links.pending)
    sector_sum = everyone(links, part.at[0], part_sector, sector, N_SECTOR, at_sector)
    rows_sum = spread(links, total, out_one, back_one, term, at_term)
    part[1] = sector_sum()
    term_sum = everyone(links, part.at[1], part_term, term, N_TERM, at_term)
    links.drain(gathered)
    coupled = rows_sum()
    sigma = [jnp.where(inside[b], diag[b] * start[b] + coupled[b], 0.0) for b in range(BLK)]
    for b in range(BLK):
        rows_f32[0, b] = sigma[b]
    arrived_f32 = along_z(links, rows_f32.at[0], lambda k: rows_f32.at[k], at)
    for b in range(BLK):
        sigma_one[b] = sigma[b]
    rayleigh = jnp.sum(term_sum(), keepdims=True) / start_squares

    def residual_here(begin, end):
        arrived_f32(begin, end)
        for k in range(begin, end):
            for h in range(2):
                before = raw_one[h, core, x, y, k].astype(F32)
                after = rows_f32[k, h * 2 : h * 2 + 2].reshape(2 * ROWS, TILE)
                raw_two[h, core, x, y, k] = (after - rayleigh * before).astype(BF16)

    squares = jnp.sum(gather(links, raw_two, vector, at, residual_here, ORDER_TWO), keepdims=True)
    scale = lax.rsqrt(squares / float(NBLK * TILE * TILE) + 1e-06)
    contract(steps_s, last_s, vector, lefts, rights, prefix, total)
    gathered = list(links.pending)
    rows_sum = spread(links, total, out_two, back_two, term, at_term)
    links.drain(gathered)
    coupled = rows_sum()
    for b in range(BLK):
        second = raw_two[b // 2, core, x, y, 0].astype(F32)[(b % 2) * ROWS : (b % 2 + 1) * ROWS]
        sigma_two[b] = jnp.where(inside[b], (diag[b] * second + coupled[b]) * scale, 0.0)
    links.drain()


def keep_kernel(one, two, one_out, two_out):
    one_out[...] = one[...]
    two_out[...] = two[...]


def body(psi, diag_energy, block_shape, *rest):
    vmem = pl.BlockSpec(memory_space=pltpu.VMEM)
    smem = pl.BlockSpec(memory_space=pltpu.SMEM)
    hbm = pl.BlockSpec(memory_space=pltpu.HBM)
    out = jax.ShapeDtypeStruct((BLK, ROWS, TILE), F32)
    raw = pltpu.VMEM((2, NCORE, NX, NY, NZ, 2 * ROWS, TILE), BF16)
    rows = pltpu.VMEM((N_TERM, 2, 2 * ROWS, TILE), BF16)
    slots = pltpu.VMEM((1, 1, PAIRS), I32)
    held = pltpu.VMEM((BLK, ROWS, TILE), F32)
    sums = pl.pallas_call(
        kernel,
        out_shape=(held, held),
        in_specs=[hbm, hbm, smem, hbm, hbm, hbm, hbm, hbm, hbm, smem],
        out_specs=(vmem, vmem),
        scratch_shapes=[
            pltpu.VMEM((2, 2 * ROWS, TILE), BF16),
            pltpu.VMEM((BLK * ROWS, TILE), F32),
            slots,
            slots,
            slots,
            slots,
            raw,
            raw,
            pltpu.VMEM((NZ, BLK, ROWS, TILE), F32),
            pltpu.VMEM((NBLK, NZ, 2 * ROWS, TILE), BF16),
            pltpu.VMEM((ENV, TILE, TILE), BF16),
            pltpu.VMEM((ENV, TILE, TILE), BF16),
            pltpu.VMEM((PAIRS + 1, TILE, TILE), BF16),
            pltpu.VMEM((BLK, TILE, TILE), F32),
            rows,
            rows,
            rows,
            rows,
            pltpu.VMEM((2, ROWS, TILE), F32),
            pltpu.VMEM((N_SECTOR, ROWS, TILE), F32),
            pltpu.VMEM((N_TERM, ROWS, TILE), F32),
            pltpu.VMEM((8, PAIRS), I32),
            pltpu.VMEM((8, TILE), I32),
            pltpu.SMEM((8, PAIRS), I32),
            pltpu.SMEM((8, TILE), I32),
            pltpu.SemaphoreType.DMA((10,)),
            pltpu.SemaphoreType.DMA((N_SEND,)),
            pltpu.SemaphoreType.DMA((N_SEND,)),
        ],
        compiler_params=pltpu.CompilerParams(
            collective_id=0, has_side_effects=True, vmem_limit_bytes=60 * 2**20
        ),
        name="two_products",
    )(psi.reshape(2, 2 * ROWS, TILE), diag_energy.reshape(BLK * ROWS, TILE), block_shape.T, *rest)
    return pl.pallas_call(
        keep_kernel,
        out_shape=(out, out),
        in_specs=[vmem, vmem],
        out_specs=(vmem, vmem),
        name="keep",
    )(*[pltpu.with_memory_space_constraint(each, pltpu.VMEM) for each in sums])


def solution(mesh):
    placed = (
        P("sector", "term", None),
        P("sector", "term", None),
        P("sector", None),
        P("term", "sector", None, None, None),
        P("term", "sector", None, None, None),
        P("term", "sector", None),
        P("term", "sector", None),
        P("term", "sector", None),
        P("term", "sector", None),
        P("term", "sector"),
    )
    return jax.shard_map(
        body,
        mesh=mesh,
        in_specs=placed,
        out_specs=(P("sector", "term", None), P("sector", "term", None)),
        check_vma=False,
    )
```
